32 devices in a mesh: lat: 4 (over y, x), lon: 8 (over z, core).
Axes of the slice: x: 2, y: 2, z: 4, core: 2. Of those that a mesh axis runs over, the one named last changes fastest.
Arguments:
- innovations: float32 [4096, 512], P(('lat', 'lon'))
- block_owner: int32 [4096, 1], P(('lat', 'lon')), may hold values from 0 to 31; in each aligned block of 128 rows (0 to 127, 128 to 255, ...) at most 8 rows name the same one
- block_lat: int32 [4096], P(('lat', 'lon')), may hold values from 0 to 124
- block_lon: int32 [4096], P(('lat', 'lon')), may hold values from 0 to 36
- block_count: int32 [32], P(('lat', 'lon')), may hold values from 1 to 128, 3584 in all
- error_weight: float32 [32, 512, 512], P(('lat', 'lon')), as said below
- courant_lon: float32 [32, 320, 512], P(None, 'lon', 'lat'), may hold values from -0.35 to 0.35
- courant_lat: float32 [32, 320, 512], P(None, 'lon', 'lat'), may hold values from -0.35 to 0.35
- background_std: float32 [32, 320, 512], P(None, 'lon', 'lat'), may hold values from 0.5 to 2
Outputs:
- solution: float32 [4096, 512], P(('lat', 'lon'))
- increment: float32 [32, 320, 512], P(None, 'lon', 'lat')
The draws below stay inside these ranges and needn't reach their ends.
Inputs may be any that keep to these rules, and one draw needn't show every extreme that they name: `block_owner`: tile index is the lat index times the number of lon devices plus the lon index. Among the 128 block slots of one device no tile is named more than 8 times, and in every draw some device names some tile exactly 8 times. Only the first block_count slots of a device hold live blocks; some device holds 128 live blocks. `block_lat`: the footprint of 4 x 4 cells lies inside the tile. `block_lon`: the footprint of 4 x 4 cells lies inside the tile. `error_weight`: one matrix for the blocks of each device.
All inputs are finite; a program needn't handle non-finite values.
Results may differ from the reference program's by a relative error of at most 0.0003.
Values sent between devices are 32-bit elements; how exact they have to be, the bound alone decides.
A program may use at most 192 MiB of HBM per device.

```python
import math
import jax
import jax.numpy as jnp
import numpy as np
from jax import lax

LEV = 32
FOOT = 4
BLOCK = 512
CLAT = 128
CLON = 40
NB = 128
STEPS = 4
ITERS = 2
CAP = 8
NLAT = 512
NLON = 320
NBLOCKS = 4096
N_LAT = 4
N_LON = 8


def draw_innovations(key, part):
    key = jax.random.fold_in(key, 11)
    device_total = NBLOCKS // NB
    holder = (jnp.arange(NBLOCKS) // NB).astype(jnp.float32)
    scaling = 1.0 + 2.0 * holder / max(device_total - 1, 1)
    base_values = jax.random.normal(key, (NBLOCKS, BLOCK), jnp.float32)
    return (base_values * scaling[:, None]).astype(jnp.float32)


def draw_error_weight(key, part):
    key = jax.random.fold_in(key, 23)
    first_key, second_key = jax.random.split(key)
    device_total = NBLOCKS // NB
    matrix_shape = (device_total, BLOCK, BLOCK)
    spread_part = jax.random.normal(first_key, matrix_shape, jnp.float32) * (0.6 / BLOCK ** 0.5)
    diagonal_part = jax.random.uniform(second_key, (device_total, BLOCK), jnp.float32, 0.7, 1.5)
    identity = (jnp.arange(BLOCK)[:, None] == jnp.arange(BLOCK)[None, :]).astype(jnp.float32)
    return (spread_part * (1.0 - identity) + identity * diagonal_part[:, :, None]).astype(jnp.float32)


def touch_ends(values, key, low, largest):
    longest = values.shape.index(max(values.shape))
    spots = []
    for shift in (0, 1):
        where = [jax.random.randint(jax.random.fold_in(key, axis), (), 0, length) for axis, length in enumerate(values.shape)]
        where[longest] = (where[longest] + shift) % values.shape[longest]
        spots.append(tuple(where))
    return values.at[spots[0]].set(low).at[spots[1]].set(largest)


def levels(key, dims, shards, least, top_value):
    def one(dim, blocks):
        heights = jax.random.uniform(jax.random.fold_in(jax.random.fold_in(key, 6), dim), (blocks,), jnp.float32, least / len(shards), top_value / len(shards))
        return jnp.repeat(jnp.exp(heights), dims[dim] // blocks).reshape((-1,) + (1,) * (len(dims) - dim - 1))

    factor_of = one(*shards[0])
    for cut in shards[1:]:
        factor_of = factor_of * one(*cut)
    return factor_of


def length_profile(amount, total, bound, lean):
    portions = [(1 << 20) // math.isqrt(rank ** lean) + 1 for rank in range(2, amount + 1)]
    surplus, holding = total - bound - (amount - 1), [1] * (amount - 1)
    while surplus > 0:
        candidates = [i for i in range(amount - 1) if holding[i] < bound]
        pool, remaining = sum([portions[i] for i in candidates]), surplus
        for i in candidates:
            more = min(bound - holding[i], max(1, remaining * portions[i] // pool), surplus)
            holding[i] = holding[i] + more
            surplus = surplus - more
    return np.array([bound] + holding)


def uneven_parts(rng, amount, total, reach, slope):
    if amount == 2:
        one = jax.random.randint(rng, (), max(1, total - reach), min(reach, total - 1) + 1)
        return jnp.stack([one, total - one])
    lengths = jnp.asarray(length_profile(amount, total, reach, slope), jnp.int32)
    pairs = (amount - 1) // 2
    donor, sink = lengths[1:1 + 2 * pairs:2], lengths[2:2 + 2 * pairs:2]
    margin = jnp.minimum(donor - 1, reach - sink)
    shifted = jax.random.randint(jax.random.fold_in(rng, 1), (pairs,), 0, 1 << 20) % (margin + 1)
    lengths = lengths.at[1:1 + 2 * pairs:2].set(donor - shifted).at[2:2 + 2 * pairs:2].set(sink + shifted)
    return lengths[jax.random.permutation(jax.random.fold_in(rng, 2), amount)]


def assign_block(own_key, own, number, rows, amount, top, most, lean):
    sequence = jax.random.permutation(own_key, amount)
    packed, ordinary = portions_of(amount, rows * top, most, lean, True), portions_of(amount, rows * top, most, lean, False)
    places = jnp.arange(amount)

    def named(tallies, rotation):
        used = int((tallies > 0).sum())
        fixed = max(1, used // 4)
        moved = fixed + (places - fixed + rotation * (used - fixed)) % max(1, amount - fixed)
        return jnp.zeros((amount,), jnp.int32).at[sequence[jnp.where(places < fixed, places, moved)]].set(jnp.asarray(tallies, jnp.int32))

    tallies = jnp.where(number % 4 == 0, named(packed, number // 4), named(ordinary, number - number // 4 - 1))
    mixed = jax.random.permutation(jax.random.fold_in(own, 3), amount)
    giver, sink = mixed[0:amount // 2 * 2:2], mixed[1:amount // 2 * 2:2]
    margin = jnp.minimum(tallies[giver] - 1, most - tallies[sink]) // 2
    margin = jnp.where((giver == sequence[0]) | (sink == sequence[0]) | (tallies[sink] == 0), 0, jnp.maximum(margin, 0))
    moved = jax.random.randint(jax.random.fold_in(own, 4), (amount // 2,), 0, 1 << 20) % (margin + 1)
    tallies = tallies.at[giver].add(-moved).at[sink].add(moved)
    labels = jnp.searchsorted(jnp.cumsum(tallies), jnp.arange(rows * top), side="right").astype(jnp.int32)
    listing = labels.reshape(top, rows).T
    listing = listing[jax.random.permutation(jax.random.fold_in(own, 1), rows)]
    rotation = jax.random.randint(jax.random.fold_in(own, 2), (rows, 1), 0, top)
    return jnp.take_along_axis(listing, (jnp.arange(top)[None, :] + rotation) % top, axis=1)


def portions_of(amount, total, reach, slope, full):
    weights = [(1 << 20) // math.isqrt(grade ** slope) + 1 for grade in range(1, amount + 1)]
    largest = reach if full else min(reach, max(-(-total // amount), total * weights[0] // sum(weights)))
    least = 1 if total - largest >= amount - 1 else 0
    counts, surplus = [largest] + [least] * (amount - 1), total - largest - least * (amount - 1)
    while surplus > 0:
        free = [i for i in range(1, amount) if counts[i] < largest] or [i for i in range(1, amount) if counts[i] < reach]
        whole, remaining = sum([weights[i] for i in free]), surplus
        for i in free:
            addition = min(reach - counts[i], max(1, remaining * weights[i] // whole), surplus)
            counts[i] = counts[i] + addition
            surplus = surplus - addition
    return np.array(counts)


def setup_inputs(seed: int = 0) -> dict:
    key_of = jax.random.split(jax.random.key(seed), 10)
    innovations = draw_innovations(jax.random.fold_in(key_of[9], 71), 0)
    block_owner_keys = jax.random.split(jax.random.fold_in(key_of[1], 1), NBLOCKS // NB)
    block_owner_turns = jax.random.permutation(jax.random.fold_in(key_of[1], 3), NBLOCKS // NB)
    block_owner = jax.vmap(lambda own, number: assign_block(jax.random.fold_in(key_of[1], 2), own, number, NB, N_LAT * N_LON, 1, CAP, 1))(block_owner_keys, block_owner_turns).reshape((NBLOCKS, 1))
    block_lat = touch_ends(jax.random.randint(key_of[2], (NBLOCKS,), 0, CLAT - FOOT + 1), jax.random.fold_in(key_of[2], 1), 0, CLAT - FOOT).astype(jnp.int32)
    block_lon = touch_ends(jax.random.randint(key_of[3], (NBLOCKS,), 0, CLON - FOOT + 1), jax.random.fold_in(key_of[3], 1), 0, CLON - FOOT).astype(jnp.int32)
    block_count = uneven_parts(key_of[4], N_LAT * N_LON, 7 * NB * N_LAT * N_LON // 8, NB, 1).astype(jnp.int32)
    error_weight = draw_error_weight(jax.random.fold_in(key_of[9], 71), 0)
    courant_lon = jnp.clip(jax.random.uniform(key_of[6], (LEV, NLON, NLAT), jnp.float32, -0.35, 0.35) * levels(key_of[6], (LEV, NLON, NLAT), ((1, 8), (2, 4)), -0.4, 0.0), -0.35, 0.35)
    courant_lat = jnp.clip(jax.random.uniform(key_of[7], (LEV, NLON, NLAT), jnp.float32, -0.35, 0.35) * levels(key_of[7], (LEV, NLON, NLAT), ((1, 8), (2, 4)), -0.4, 0.0), -0.35, 0.35)
    background_std = jnp.clip(jnp.exp(math.log(2.0) - 1.3862944 * jax.random.uniform(key_of[8], (LEV, NLON, NLAT), jnp.float32) ** levels(key_of[8], (LEV, NLON, NLAT), ((1, 8), (2, 4)), -0.2, 0.2)), 0.5, 2.0)
    return dict(innovations=innovations, block_owner=block_owner, block_lat=block_lat, block_lon=block_lon, block_count=block_count, error_weight=error_weight, courant_lon=courant_lon, courant_lat=courant_lat, background_std=background_std)


DIFFUSION = 0.15
PRECISE = lax.Precision.HIGHEST


def coefficients(courant_lon, courant_lat):
    centre = jnp.zeros_like(courant_lon) + (1.0 - 4.0 * DIFFUSION)
    return (centre, DIFFUSION - 0.5 * courant_lon, DIFFUSION + 0.5 * courant_lon,
            DIFFUSION - 0.5 * courant_lat, DIFFUSION + 0.5 * courant_lat)


def lat_next(values):
    return jnp.concatenate([values[:, :, 1:], jnp.zeros_like(values[:, :, :1])], axis=2)


def lat_prior(values):
    return jnp.concatenate([jnp.zeros_like(values[:, :, :1]), values[:, :, :-1]], axis=2)


def forward_step(field_now, weights_five):
    return (weights_five[0] * field_now + weights_five[1] * jnp.roll(field_now, -1, axis=1)
            + weights_five[2] * jnp.roll(field_now, 1, axis=1)
            + weights_five[3] * lat_next(field_now) + weights_five[4] * lat_prior(field_now))


def adjoint_step(field_now, weights_five):
    return (weights_five[0] * field_now + jnp.roll(weights_five[1] * field_now, 1, axis=1)
            + jnp.roll(weights_five[2] * field_now, -1, axis=1)
            + lat_prior(weights_five[3] * field_now) + lat_next(weights_five[4] * field_now))


def reference(innovations, block_owner, block_lat, block_lon, block_count, error_weight, courant_lon, courant_lat, background_std):
    weights_five = coefficients(courant_lon, courant_lat)
    variance = background_std * background_std
    block_index = jnp.arange(NBLOCKS, dtype=jnp.int32)
    is_live = ((block_index % NB) < block_count[block_index // NB]).astype(jnp.float32)[:, None]
    owners = block_owner[:, 0]
    offsets = jnp.arange(FOOT, dtype=jnp.int32)
    lon_cells = (owners % N_LON) * CLON + block_lon
    lat_cells = (owners // N_LON) * CLAT + block_lat
    cell_index = ((lon_cells[:, None, None] + offsets[None, :, None]) * NLAT
                  + lat_cells[:, None, None] + offsets[None, None, :]).reshape(-1)

    def weigh(block_rows):
        return jnp.einsum("dij,dnj->dni", error_weight, block_rows.reshape(-1, NB, BLOCK), precision=PRECISE).reshape(NBLOCKS, BLOCK)

    def weigh_transposed(block_rows):
        return jnp.einsum("dji,dnj->dni", error_weight, block_rows.reshape(-1, NB, BLOCK), precision=PRECISE).reshape(NBLOCKS, BLOCK)

    def adjoint_spread(dual_rows):
        patches = weigh_transposed(dual_rows).reshape(NBLOCKS, LEV, FOOT * FOOT).transpose(1, 0, 2).reshape(LEV, -1)
        field_now = jnp.zeros((LEV, NLON * NLAT), jnp.float32).at[:, cell_index].add(patches).reshape(LEV, NLON, NLAT)
        for step_index in range(STEPS):
            field_now = adjoint_step(field_now, weights_five)
        return variance * field_now

    def apply_system(direction):
        field_now = adjoint_spread(direction)
        for step_index in range(STEPS):
            field_now = forward_step(field_now, weights_five)
        picked = field_now.reshape(LEV, -1)[:, cell_index].reshape(LEV, NBLOCKS, FOOT * FOOT)
        picked = picked.transpose(1, 0, 2).reshape(NBLOCKS, BLOCK) * is_live
        return direction + weigh(picked)

    right_side = weigh(innovations) * is_live
    solution = jnp.zeros_like(right_side)
    residual = right_side
    direction = right_side
    norm_now = jnp.sum(residual * residual)
    for iter_index in range(ITERS):
        image = apply_system(direction)
        step_size = norm_now / jnp.sum(direction * image)
        solution = solution + step_size * direction
        residual = residual - step_size * image
        norm_next = jnp.sum(residual * residual)
        direction = residual + (norm_next / norm_now) * direction
        norm_now = norm_next
    return solution, adjoint_spread(solution)
```

```python
import jax
import jax.numpy as jnp
from jax import lax
from jax.sharding import PartitionSpec as P

LEV = 32
FOOT = 4
STEPS = 4
ITERS = 2


DIFFUSION = 0.15
PRECISE = lax.Precision.HIGHEST


def with_halo(array, sides, width, wrap):
    for axis, dim in sides:
        count, length = (lax.axis_size(axis), array.shape[dim])
        up = [(i, (i + 1) % count) for i in range(count if wrap else count - 1)]
        down = [(j, i) for i, j in up]
        last = lax.slice_in_dim(array, length - width, length, axis=dim)
        leading = lax.slice_in_dim(array, 0, width, axis=dim)
        before = lax.ppermute(last, axis, up)
        after = lax.ppermute(leading, axis, down)
        array = jnp.concatenate([before, array, after], axis=dim)
    return array


def extend(values, halo_width):
    flattened = values.reshape((-1,) + values.shape[-2:])
    flattened = with_halo(flattened, (("lon", 1),), halo_width, True)
    flattened = with_halo(flattened, (("lat", 2),), halo_width, False)
    return flattened.reshape(values.shape[:-2] + flattened.shape[-2:])


def stencil(padded, stencil_weights, halo_width):
    margin_cut = STEPS - halo_width + 1
    local_weights = stencil_weights[
        :,
        :,
        margin_cut : stencil_weights.shape[2] - margin_cut,
        margin_cut : stencil_weights.shape[3] - margin_cut,
    ]
    return (
        local_weights[0] * padded[:, 1:-1, 1:-1]
        + local_weights[1] * padded[:, 2:, 1:-1]
        + local_weights[2] * padded[:, :-2, 1:-1]
        + local_weights[3] * padded[:, 1:-1, 2:]
        + local_weights[4] * padded[:, 1:-1, :-2]
    )


def propagate(field_now, stencil_weights):
    for step_index in range(STEPS):
        field_now = stencil(extend(field_now, 1), stencil_weights, 1)
    return field_now


def trade_blocks(slot_rows, slot_depth):
    lat_count = lax.axis_size("lat")
    lon_count = lax.axis_size("lon")
    row_width = slot_rows.shape[-1]
    direct = slot_rows.reshape(lat_count * lon_count, slot_depth, row_width)
    arrived = lax.all_to_all(direct, ("lat", "lon"), split_axis=0, concat_axis=0, tiled=True)
    return arrived.reshape(lat_count * lon_count * slot_depth, row_width)


def pack_rows(block_rows, target, total_slots):
    holder = jnp.zeros((total_slots + 1, block_rows.shape[1]), block_rows.dtype)
    return holder.at[target].set(block_rows)[:total_slots]


def unpack_rows(slot_rows, target):
    padded = jnp.concatenate([slot_rows, jnp.zeros_like(slot_rows[:1])], axis=0)
    return padded[target]


def sample_field(field_now, cell_index, slot_total):
    picked = field_now.reshape(field_now.shape[0], -1)[:, cell_index]
    picked = picked.reshape(field_now.shape[0], slot_total, FOOT * FOOT)
    return picked.transpose(1, 0, 2).reshape(slot_total, -1)


def spread_rows(slot_rows, cell_index, field_shape):
    patches = (
        slot_rows.reshape(slot_rows.shape[0], LEV, FOOT * FOOT).transpose(1, 0, 2).reshape(LEV, -1)
    )
    flat_field = (
        jnp.zeros((LEV, field_shape[1] * field_shape[2]), jnp.float32)
        .at[:, cell_index]
        .add(patches)
    )
    return flat_field.reshape(field_shape)


def squares(residual):
    return lax.psum(jnp.sum(residual * residual), ("lat", "lon"))


def body(
    innovations,
    block_owner,
    block_lat,
    block_lon,
    block_count,
    error_weight,
    courant_lon,
    courant_lat,
    background_std,
):
    matrix = error_weight[0]
    block_total = innovations.shape[0]
    device_total = lax.axis_size("lat") * lax.axis_size("lon")
    slot_depth = 2 * block_total // device_total
    total_slots = device_total * slot_depth
    field_shape = courant_lon.shape
    is_live = jnp.arange(block_total) < block_count[0]
    owners = block_owner[:, 0]
    onehot = ((owners[:, None] == jnp.arange(device_total)[None, :]) & is_live[:, None]).astype(
        jnp.int32
    )
    before = jnp.sum((jnp.cumsum(onehot, axis=0) - onehot) * onehot, axis=1)
    target = jnp.where(is_live, owners * slot_depth + before, total_slots)
    anchor_rows = jnp.stack([block_lon, block_lat], axis=1)
    anchor_slots = pack_rows(anchor_rows, target, total_slots).reshape(device_total, slot_depth, 2)
    anchors = lax.all_to_all(
        anchor_slots, ("lat", "lon"), split_axis=0, concat_axis=0, tiled=True
    ).reshape(total_slots, 2)
    offsets = jnp.arange(FOOT, dtype=jnp.int32)
    cell_index = (
        (anchors[:, 0][:, None, None] + offsets[None, :, None]) * field_shape[2]
        + anchors[:, 1][:, None, None]
        + offsets[None, None, :]
    ).reshape(-1)
    centre = jnp.zeros_like(courant_lon) + (1.0 - 4.0 * DIFFUSION)
    raw_weights = jnp.stack(
        [
            centre,
            DIFFUSION - 0.5 * courant_lon,
            DIFFUSION + 0.5 * courant_lon,
            DIFFUSION - 0.5 * courant_lat,
            DIFFUSION + 0.5 * courant_lat,
        ]
    )
    wide_weights = extend(raw_weights, STEPS + 1)
    forward_weights = wide_weights[:, :, 1:-1, 1:-1]
    lat_first = lax.axis_index("lat") * field_shape[2] - STEPS
    lat_global = lat_first + jnp.arange(field_shape[2] + 2 * STEPS)
    inside = ((lat_global >= 0) & (lat_global < field_shape[2] * lax.axis_size("lat"))).astype(
        jnp.float32
    )
    adjoint_weights = (
        jnp.stack(
            [
                wide_weights[0, :, 1:-1, 1:-1],
                wide_weights[2, :, 2:, 1:-1],
                wide_weights[1, :, :-2, 1:-1],
                wide_weights[4, :, 1:-1, 2:],
                wide_weights[3, :, 1:-1, :-2],
            ]
        )
        * inside
    )
    variance = background_std * background_std

    def propagate_rows(dual_rows):
        weighted = jnp.dot(dual_rows, matrix, precision=PRECISE)
        arrived = trade_blocks(pack_rows(weighted, target, total_slots), slot_depth)
        return propagate(spread_rows(arrived, cell_index, field_shape), adjoint_weights)

    right_side = jnp.dot(innovations, matrix.T, precision=PRECISE) * is_live[:, None].astype(
        jnp.float32
    )
    norm_first = squares(right_side)
    first = propagate_rows(right_side)
    energy = jnp.sum(first * variance * first)
    step_first = norm_first / (norm_first + lax.psum(energy, ("lat", "lon")))
    model_state = propagate(variance * first, forward_weights)
    returned = trade_blocks(sample_field(model_state, cell_index, total_slots), slot_depth)
    image = right_side + jnp.dot(unpack_rows(returned, target), matrix.T, precision=PRECISE)
    residual = right_side - step_first * image
    norm_next = squares(residual)
    ratio = norm_next / norm_first
    direction = residual + ratio * right_side
    second = propagate_rows(residual) + ratio * first
    energy = jnp.sum(direction * direction) + jnp.sum(second * variance * second)
    step_second = norm_next / lax.psum(energy, ("lat", "lon"))
    solution = step_first * right_side + step_second * direction
    return (solution, variance * (step_first * first + step_second * second))


def solution(mesh):
    in_specs = (
        P(("lat", "lon"), None),
        P(("lat", "lon"), None),
        P(("lat", "lon")),
        P(("lat", "lon")),
        P(("lat", "lon")),
        P(("lat", "lon"), None, None),
        P(None, "lon", "lat"),
        P(None, "lon", "lat"),
        P(None, "lon", "lat"),
    )
    out_specs = (P(("lat", "lon"), None), P(None, "lon", "lat"))
    return jax.shard_map(body, mesh=mesh, in_specs=in_specs, out_specs=out_specs, check_vma=False)
```

```python
import functools

import jax
import jax.numpy as jnp
from jax import lax
from jax.experimental import pallas as pl
from jax.experimental.pallas import tpu as pltpu
from jax.sharding import PartitionSpec as P

FOOT = 4
STEPS = 4
DIFFUSION = 0.15
CENTRE = 1.0 - 4.0 * DIFFUSION
PRECISE = lax.Precision.HIGHEST
MESH = pl.DeviceIdType.MESH
LANES = 128
DEPTH = 8
HLON = 8
HROW = 2
LIMIT = 48 * 1024 * 1024


def place():
    lat_n, lon_n = lax.axis_size("lat"), lax.axis_size("lon")
    lat_i, lon_i = lax.axis_index("lat"), lax.axis_index("lon")
    return lat_n, lon_n, lat_i, lon_i


def greet_all():
    lat_n, lon_n, lat_i, lon_i = place()
    total = lat_n * lon_n
    me = lat_i * lon_n + lon_i
    barrier = pltpu.get_barrier_semaphore()

    def greet(d, carry):
        peer = lax.rem(me + d, total)
        pl.semaphore_signal(
            barrier, inc=1, device_id=(lax.div(peer, lon_n), lax.rem(peer, lon_n)), device_id_type=MESH
        )
        return carry

    lax.fori_loop(1, total, greet, 0)
    pl.semaphore_wait(barrier, total - 1)


def greet_near():
    lat_n, lon_n, lat_i, lon_i = place()
    barrier = pltpu.get_barrier_semaphore()
    for near in (lax.rem(lon_i + 1, lon_n), lax.rem(lon_i + lon_n - 1, lon_n)):
        pl.semaphore_signal(barrier, inc=1, device_id=(lat_i, near), device_id_type=MESH)

    @pl.when(lat_i > 0)
    def _():
        pl.semaphore_signal(barrier, inc=1, device_id=(lat_i - 1, lon_i), device_id_type=MESH)

    @pl.when(lat_i < lat_n - 1)
    def _():
        pl.semaphore_signal(barrier, inc=1, device_id=(lat_i + 1, lon_i), device_id_type=MESH)

    peers = 2 + jnp.where(lat_i > 0, 1, 0) + jnp.where(lat_i < lat_n - 1, 1, 0)
    pl.semaphore_wait(barrier, peers)


def trade_copy(sent, got, send_sems, recv_sems, peer, slot, lon_n):
    return pltpu.make_async_remote_copy(
        src_ref=sent.at[peer],
        dst_ref=got.at[slot],
        send_sem=send_sems.at[peer],
        recv_sem=recv_sems.at[slot],
        device_id=(lax.div(peer, lon_n), lax.rem(peer, lon_n)),
        device_id_type=MESH,
    )


def trade_start(sent, got, send_sems, recv_sems):
    lat_n, lon_n, lat_i, lon_i = place()
    total = lat_n * lon_n
    me = lat_i * lon_n + lon_i

    def send(d, carry):
        peer = lax.rem(me + d, total)
        trade_copy(sent, got, send_sems, recv_sems, peer, me, lon_n).start()
        return carry

    lax.fori_loop(1, total, send, 0)
    got[me] = sent[me]


def trade_wait(sent, got, send_sems, recv_sems):
    lat_n, lon_n, lat_i, lon_i = place()
    total = lat_n * lon_n
    me = lat_i * lon_n + lon_i

    def finish(d, carry):
        peer = lax.rem(me + d, total)
        copy = trade_copy(sent, got, send_sems, recv_sems, peer, peer, lon_n)
        copy.wait_send()
        copy.wait_recv()
        return carry

    lax.fori_loop(1, total, finish, 0)


def part(ref, rows, columns):
    if len(ref.shape) == 4:
        return ref.at[:, pl.ds(*rows), pl.ds(*columns)]
    return ref.at[pl.ds(*rows), pl.ds(*columns)]


def halo_copies(wide, send_sems, recv_sems):
    lat_n, lon_n, lat_i, lon_i = place()
    rows, columns = wide.shape[-3], wide.shape[-2]
    inner = (HLON, columns - 2 * HLON)

    def copy(index, source, target, device):
        return pltpu.make_async_remote_copy(
            src_ref=source,
            dst_ref=target,
            send_sem=send_sems.at[index],
            recv_sem=recv_sems.at[index],
            device_id=device,
            device_id_type=MESH,
        )

    down = copy(0, part(wide, (HROW, HROW), inner), part(wide, (rows - HROW, HROW), inner), (lat_i - 1, lon_i))
    up = copy(1, part(wide, (rows - 2 * HROW, HROW), inner), part(wide, (0, HROW), inner), (lat_i + 1, lon_i))
    west = copy(
        2,
        part(wide, (0, rows), (HLON, HLON)),
        part(wide, (0, rows), (columns - HLON, HLON)),
        (lat_i, lax.rem(lon_i + lon_n - 1, lon_n)),
    )
    east = copy(
        3,
        part(wide, (0, rows), (columns - 2 * HLON, HLON)),
        part(wide, (0, rows), (0, HLON)),
        (lat_i, lax.rem(lon_i + 1, lon_n)),
    )
    return down, up, west, east


def lat_edges(wide):
    lat_n, lon_n, lat_i, lon_i = place()
    rows = wide.shape[-3]
    for ends, first in ((lat_i == 0, 0), (lat_i == lat_n - 1, rows - HROW)):

        @pl.when(ends)
        def _(first=first):
            if len(wide.shape) == 4:
                for index in range(wide.shape[0]):
                    for row in range(HROW):
                        wide[index, first + row] = jnp.zeros(wide.shape[2:], jnp.float32)
            else:
                for row in range(HROW):
                    wide[first + row] = jnp.zeros(wide.shape[1:], jnp.float32)


def lat_start(down, up):
    lat_n, lon_n, lat_i, lon_i = place()

    @pl.when(lat_i > 0)
    def _():
        down.start()

    @pl.when(lat_i < lat_n - 1)
    def _():
        up.start()


def lat_wait(down, up):
    lat_n, lon_n, lat_i, lon_i = place()

    @pl.when(lat_i > 0)
    def _():
        down.wait_send()
        up.wait_recv()

    @pl.when(lat_i < lat_n - 1)
    def _():
        up.wait_send()
        down.wait_recv()


def dot(left, right, axes=((1,), (0,))):
    return lax.dot_general(
        left, right, (axes, ((), ())), precision=PRECISE, preferred_element_type=jnp.float32
    )


def full_sum(values):
    return jnp.sum(jnp.sum(values, axis=0, keepdims=True), axis=1, keepdims=True)


def gathered_sum(got, first, lane_index):
    tile = jnp.sum(got[:, :, first : first + LANES], axis=0)
    lane = lax.broadcasted_iota(jnp.int32, tile.shape, 1)
    row = lax.broadcasted_iota(jnp.int32, tile.shape, 0)
    return full_sum(jnp.where((lane == lane_index) & (row == 0), tile, 0.0))


def first_kernel(
    count, owner, spot, innovations, matrix, fields,
    rows_out, anchors_out, permuted, residual, packing, norm_out, wide,
    sent, got, send_sems, recv_sems, halo_send, halo_recv,
):
    slots, block_total = packing.shape
    total = slots // DEPTH
    width = matrix.shape[0]
    field_rows, field_columns = fields.shape[1], fields.shape[2]

    def fill(row, carry):
        for index in range(3):
            wide[index, HROW + row, pl.ds(HLON, field_columns)] = fields[index, row]
        return carry

    lax.fori_loop(0, field_rows, fill, 0)
    lat_edges(wide)
    down, up, west, east = halo_copies(wide, halo_send, halo_recv)
    greet_all()
    lat_start(down, up)

    live_column = lax.broadcasted_iota(jnp.int32, (block_total, 1), 0) < count[0]
    start = jnp.where(live_column, dot(innovations[...], matrix[...], ((1,), (1,))), 0.0)
    residual[...] = start
    row = lax.broadcasted_iota(jnp.int32, (width, width), 0)
    column = lax.broadcasted_iota(jnp.int32, (width, width), 1)
    footprint = FOOT * FOOT
    shuffle = column == lax.rem(row, footprint) * (width // footprint) + lax.div(row, footprint)
    permuted[...] = dot(matrix[...], shuffle.astype(jnp.float32))
    weighted = dot(start, permuted[...])

    live_row = lax.broadcasted_iota(jnp.int32, (1, block_total), 1) < count[0]
    owners = owner[...]
    tiles = lax.broadcasted_iota(jnp.int32, (total, block_total), 0)
    named = jnp.where((tiles == owners) & live_row, 1.0, 0.0)
    earlier = lax.broadcasted_iota(jnp.int32, (block_total, block_total), 0) < lax.broadcasted_iota(
        jnp.int32, (block_total, block_total), 1
    )
    ranks = jnp.sum(named * dot(named, earlier.astype(jnp.float32)), axis=0, keepdims=True)
    target = owners.astype(jnp.float32) * DEPTH + ranks
    slot_ids = lax.broadcasted_iota(jnp.int32, (slots, block_total), 0).astype(jnp.float32)
    pack = jnp.where((slot_ids == target) & live_row, 1.0, 0.0)
    packing[...] = pack
    sent[:, :, :width] = dot(pack, weighted).reshape(total, DEPTH, width)
    lane = lax.broadcasted_iota(jnp.int32, (slots, LANES), 1)
    spots = jnp.where(lane == 2, full_sum(start * start), dot(pack, spot[...]))
    sent[:, :, width:] = spots.reshape(total, DEPTH, LANES)
    trade_start(sent, got, send_sems, recv_sems)
    lat_wait(down, up)
    west.start()
    east.start()
    trade_wait(sent, got, send_sems, recv_sems)
    unload(got, rows_out)
    anchors_out[...] = got[:, :, width:].reshape(slots, LANES)
    norm_out[...] = jnp.broadcast_to(gathered_sum(got, width, 2), norm_out.shape)
    west.wait()
    east.wait()


def unload(got, rows_out):
    slots, groups = rows_out.shape[:2]
    for group in range(groups):
        rows_out[:, group, :] = got[:, :, group * LANES : (group + 1) * LANES].reshape(slots, LANES)


def spread_kernel(anchors, rows, field):
    slots = rows.shape[0]
    level_lanes = LANES // FOOT
    field[...] = jnp.zeros(field.shape, jnp.float32)

    def add(slot, carry):
        column, latitude = anchors[slot], anchors[slots + slot]
        row, shift = lax.div(latitude, FOOT), lax.rem(latitude, FOOT) * level_lanes
        patch = pltpu.roll(rows[slot], shift, 1)
        lane = lax.broadcasted_iota(jnp.int32, patch.shape, 1)
        here = lane >= shift
        field[row, pl.ds(column, FOOT), :] += jnp.where(here, patch, 0.0)
        field[row + 1, pl.ds(column, FOOT), :] += jnp.where(here, 0.0, patch)
        return carry

    lax.fori_loop(0, slots, add, 0, unroll=4)


def sample_kernel(anchors, field, rows):
    slots = rows.shape[0]
    level_lanes = LANES // FOOT

    def pick(slot, carry):
        column, latitude = anchors[slot], anchors[slots + slot]
        row, shift = lax.div(latitude, FOOT), lax.rem(latitude, FOOT) * level_lanes
        here = field[row, pl.ds(column, FOOT), :]
        after = field[row + 1, pl.ds(column, FOOT), :]
        lane = lax.broadcasted_iota(jnp.int32, here.shape, 1)
        rows[slot] = pltpu.roll(jnp.where(lane >= shift, here, after), lax.rem(LANES - shift, LANES), 1)
        return carry

    lax.fori_loop(0, slots, pick, 0, unroll=8)


def model_step(now, later, wide, adjoint):
    lat_n, lon_n, lat_i, lon_i = place()
    rows, columns = now.shape[0], now.shape[1]
    level_lanes = LANES // FOOT
    low = jnp.where(lat_i > 0, 1.0, 0.0)
    high = jnp.where(lat_i < lat_n - 1, 1.0, 0.0)
    lane = lax.broadcasted_iota(jnp.int32, (columns, LANES), 1)
    first, last = lane < level_lanes, lane >= LANES - level_lanes

    def plane(row, carry):
        before, after = lax.rem(row + rows - 1, rows), lax.rem(row + 1, rows)
        here = now[row]
        prior = jnp.where(last, now[before], here)
        following = jnp.where(first, now[after], here)
        zonal, meridional = 0.5 * wide[0, row], wide[1, row]
        if adjoint:
            prior_wind = jnp.where(last, wide[1, before], meridional)
            next_wind = jnp.where(first, wide[1, after], meridional)
            value = (
                CENTRE * here
                + pltpu.roll((DIFFUSION - zonal) * here, 1, 0)
                + pltpu.roll((DIFFUSION + zonal) * here, columns - 1, 0)
                + pltpu.roll((DIFFUSION - 0.5 * prior_wind) * prior, level_lanes, 1)
                + pltpu.roll((DIFFUSION + 0.5 * next_wind) * following, LANES - level_lanes, 1)
            )
        else:
            value = (
                CENTRE * here
                + (DIFFUSION - zonal) * pltpu.roll(here, columns - 1, 0)
                + (DIFFUSION + zonal) * pltpu.roll(here, 1, 0)
                + (DIFFUSION - 0.5 * meridional) * pltpu.roll(following, LANES - level_lanes, 1)
                + (DIFFUSION + 0.5 * meridional) * pltpu.roll(prior, level_lanes, 1)
            )
        keep = jnp.where(row < HROW, low, jnp.where(row >= rows - HROW, high, 1.0))
        later[row] = value * keep
        return carry

    lax.fori_loop(0, rows, plane, 0)


def model_steps(held, other, wide, adjoint):
    def pair(index, carry):
        model_step(held, other, wide, adjoint)
        model_step(other, held, wide, adjoint)
        return carry

    lax.fori_loop(0, STEPS // 2, pair, 0)


def load_wide(field, held, send_sems, recv_sems, greet):
    columns = field.shape[1]

    def fill(row, carry):
        held[HROW + row, pl.ds(HLON, columns)] = field[row]
        return carry

    lax.fori_loop(0, held.shape[0] - 2 * HROW, fill, 0)
    lat_edges(held)
    down, up, west, east = halo_copies(held, send_sems, recv_sems)
    greet()
    lat_start(down, up)
    lat_wait(down, up)
    west.start()
    east.start()
    west.wait()
    east.wait()


def system_kernel(field, wide, adjoint_out, forward_out, energy_out, held, other, send_sems, recv_sems):
    rows, columns = held.shape[0], held.shape[1]
    own = columns - 2 * HLON
    load_wide(field, held, send_sems, recv_sems, greet_near)
    model_steps(held, other, wide, True)

    def scale(row, energy):
        value, deviation = held[row], wide[2, row]
        scaled = deviation * deviation * value
        held[row] = scaled
        adjoint_out[row - HROW] = value[HLON : HLON + own]
        return energy + (scaled * value)[HLON : HLON + own]

    energy = lax.fori_loop(HROW, rows - HROW, scale, jnp.zeros((own, LANES), jnp.float32))
    energy_out[...] = jnp.broadcast_to(full_sum(energy), energy_out.shape)
    for row in (*range(HROW), *range(rows - HROW, rows)):
        deviation = wide[2, row]
        held[row] = deviation * deviation * held[row]
    model_steps(held, other, wide, False)

    def write(row, carry):
        forward_out[row] = held[HROW + row, pl.ds(HLON, own)]
        return carry

    lax.fori_loop(0, rows - 2 * HROW, write, 0)
    forward_out[rows - 2 * HROW] = jnp.zeros((own, LANES), jnp.float32)


def return_kernel(
    rows, energy, matrix, start, packing, norm,
    rows_out, direction, step_out, ratio_out, norm_out, square_out,
    sent, got, sent_next, got_next, send_sems, recv_sems, send_next, recv_next,
):
    slots, groups = rows.shape[:2]
    total = slots // DEPTH
    width = matrix.shape[0]
    for group in range(groups):
        sent[:, :, group * LANES : (group + 1) * LANES] = rows[:, group, :].reshape(total, DEPTH, LANES)
    sent[:, :, width:] = jnp.broadcast_to(energy[...][None], (total, DEPTH, LANES))
    greet_all()
    trade_start(sent, got, send_sems, recv_sems)
    trade_wait(sent, got, send_sems, recv_sems)
    norm_first = norm[0:1, 0:1]
    step = norm_first / (norm_first + gathered_sum(got, width, 0))
    back = dot(packing[...], got[:, :, :width].reshape(slots, width), ((0,), (0,)))
    image = start[...] + dot(back, matrix[...], ((1,), (1,)))
    residual = start[...] - step * image
    pack = packing[...]
    sent_next[:, :, :width] = dot(pack, dot(residual, matrix[...])).reshape(total, DEPTH, width)
    sent_next[:, :, width:] = jnp.broadcast_to(full_sum(residual * residual)[None], (total, DEPTH, LANES))
    trade_start(sent_next, got_next, send_next, recv_next)
    trade_wait(sent_next, got_next, send_next, recv_next)
    unload(got_next, rows_out)
    norm_next = gathered_sum(got_next, width, 0)
    ratio = norm_next / norm_first
    moved = residual + ratio * start[...]
    direction[...] = moved
    step_out[...] = jnp.broadcast_to(step, step_out.shape)
    ratio_out[...] = jnp.broadcast_to(ratio, ratio_out.shape)
    norm_out[...] = jnp.broadcast_to(norm_next, norm_out.shape)
    square_out[...] = jnp.broadcast_to(full_sum(moved * moved), square_out.shape)


def last_kernel(
    field, wide, earlier, ratio, norm, square,
    adjoint_out, step_out,
    held, other, sent, got, halo_send, halo_recv, send_sems, recv_sems,
):
    rows, columns = held.shape[0], held.shape[1]
    own = columns - 2 * HLON
    load_wide(field, held, halo_send, halo_recv, greet_all)
    model_steps(held, other, wide, True)
    scale = ratio[0:1, 0:1]

    def combine(row, energy):
        value = held[HROW + row, pl.ds(HLON, own)] + scale * earlier[row]
        adjoint_out[row] = value
        deviation = wide[2, HROW + row, pl.ds(HLON, own)] * value
        return energy + deviation * deviation

    energy = lax.fori_loop(0, rows - 2 * HROW, combine, jnp.zeros((own, LANES), jnp.float32))
    sent[...] = jnp.broadcast_to((full_sum(energy) + square[0:1, 0:1])[None], sent.shape)
    trade_start(sent, got, send_sems, recv_sems)
    trade_wait(sent, got, send_sems, recv_sems)
    step_out[...] = jnp.broadcast_to(norm[0:1, 0:1] / gathered_sum(got, 0, 0), step_out.shape)


def vmem(count):
    return [pl.BlockSpec(memory_space=pltpu.VMEM)] * count


def smem():
    return pl.BlockSpec(memory_space=pltpu.SMEM)


def shape(*sizes):
    return jax.ShapeDtypeStruct(sizes, jnp.float32)


def params(collective_id=None):
    if collective_id is None:
        return pltpu.CompilerParams(vmem_limit_bytes=LIMIT)
    return pltpu.CompilerParams(
        collective_id=collective_id, has_side_effects=True, vmem_limit_bytes=LIMIT
    )


def folded(values):
    levels, columns, latitudes = values.shape
    return (
        values.reshape(levels, columns, latitudes // FOOT, FOOT)
        .transpose(2, 1, 3, 0)
        .reshape(latitudes // FOOT, columns, FOOT * levels)
    )


def unfolded(values, levels):
    rows, columns, _ = values.shape
    return values.reshape(rows, columns, FOOT, levels).transpose(3, 1, 0, 2).reshape(levels, columns, rows * FOOT)


def body(
    innovations, block_owner, block_lat, block_lon, block_count,
    error_weight, courant_lon, courant_lat, background_std,
):
    total = lax.axis_size("lat") * lax.axis_size("lon")
    block_total, width = innovations.shape
    levels, columns, latitudes = courant_lon.shape
    rows = latitudes // FOOT
    slots = total * DEPTH
    groups = width // LANES
    wide_rows, wide_columns = rows + 2 * HROW, columns + 2 * HLON
    fields = jnp.stack([folded(courant_lon), folded(courant_lat), folded(background_std)])
    spot = jnp.pad(
        jnp.stack([block_lon, block_lat], axis=1).astype(jnp.float32), ((0, 0), (0, LANES - 2))
    )
    tile = shape(DEPTH, LANES)
    chunks = pltpu.VMEM((total, DEPTH, width + LANES), jnp.float32)
    dma = pltpu.SemaphoreType.DMA

    arrived, anchors, matrix, start, packing, norm, wide = pl.pallas_call(
        first_kernel,
        out_shape=(
            shape(slots, groups, LANES), shape(slots, LANES), shape(width, width),
            shape(block_total, width), shape(slots, block_total), tile,
            shape(3, wide_rows, wide_columns, LANES),
        ),
        in_specs=[smem()] + vmem(5),
        out_specs=tuple(vmem(7)),
        scratch_shapes=[chunks, chunks, dma((total,)), dma((total,)), dma((4,)), dma((4,))],
        compiler_params=params(0),
    )(block_count, block_owner.reshape(1, block_total), spot, innovations, error_weight[0], fields)

    corners = jnp.concatenate([anchors[:, 0], anchors[:, 1]]).astype(jnp.int32)

    def spread(block_rows):
        return pl.pallas_call(
            spread_kernel,
            out_shape=shape(rows + 1, columns, LANES),
            in_specs=[smem()] + vmem(1),
            out_specs=vmem(1)[0],
            compiler_params=params(),
        )(corners, block_rows)

    held = pltpu.VMEM((wide_rows, wide_columns, LANES), jnp.float32)
    first, model_state, energy = pl.pallas_call(
        system_kernel,
        out_shape=(shape(rows, columns, LANES), shape(rows + 1, columns, LANES), tile),
        in_specs=vmem(2),
        out_specs=tuple(vmem(3)),
        scratch_shapes=[held, held, dma((4,)), dma((4,))],
        compiler_params=params(1),
    )(spread(arrived), wide)

    picked = pl.pallas_call(
        sample_kernel,
        out_shape=shape(slots, groups, LANES),
        in_specs=[smem()] + vmem(1),
        out_specs=vmem(1)[0],
        compiler_params=params(),
    )(corners, model_state)

    arrived, direction, step_first, ratio, norm_next, square = pl.pallas_call(
        return_kernel,
        out_shape=(shape(slots, groups, LANES), shape(block_total, width), tile, tile, tile, tile),
        in_specs=vmem(6),
        out_specs=tuple(vmem(6)),
        scratch_shapes=[chunks, chunks, chunks, chunks] + [dma((total,))] * 4,
        compiler_params=params(2),
    )(picked, energy, matrix, start, packing, norm)

    tiles = pltpu.VMEM((total, DEPTH, LANES), jnp.float32)
    second, step_second = pl.pallas_call(
        last_kernel,
        out_shape=(shape(rows, columns, LANES), tile),
        in_specs=vmem(6),
        out_specs=tuple(vmem(2)),
        scratch_shapes=[held, held, tiles, tiles, dma((4,)), dma((4,)), dma((total,)), dma((total,))],
        compiler_params=params(3),
    )(spread(arrived), wide, first, ratio, norm_next, square)

    step_first, step_second = step_first[0, 0], step_second[0, 0]
    solution = step_first * start + step_second * direction
    increment = unfolded(step_first * first + step_second * second, levels)
    return solution, background_std * background_std * increment


def solution(mesh):
    blocks = P(("lat", "lon"))
    in_specs = (
        P(("lat", "lon"), None),
        P(("lat", "lon"), None),
        blocks,
        blocks,
        blocks,
        P(("lat", "lon"), None, None),
        P(None, "lon", "lat"),
        P(None, "lon", "lat"),
        P(None, "lon", "lat"),
    )
    out_specs = (P(("lat", "lon"), None), P(None, "lon", "lat"))
    return jax.shard_map(body, mesh=mesh, in_specs=in_specs, out_specs=out_specs, check_vma=False)
```

```python
import functools

import jax
import jax.numpy as jnp
from jax import lax
from jax.experimental import pallas as pl
from jax.experimental.pallas import tpu as pltpu
from jax.sharding import PartitionSpec as P

FOOT = 4
STEPS = 4
DIFFUSION = 0.15
CENTRE = 1.0 - 4.0 * DIFFUSION
PRECISE = lax.Precision.HIGHEST
MESH = pl.DeviceIdType.MESH
LANES = 128
DEPTH = 8
HLON = 8
HROW = 2
LIMIT = 48 * 1024 * 1024


def place():
    lat_n, lon_n = lax.axis_size("lat"), lax.axis_size("lon")
    lat_i, lon_i = lax.axis_index("lat"), lax.axis_index("lon")
    return lat_n, lon_n, lat_i, lon_i


def signal_all():
    lat_n, lon_n, lat_i, lon_i = place()
    total = lat_n * lon_n
    me = lat_i * lon_n + lon_i
    barrier = pltpu.get_barrier_semaphore()

    def greet(d, carry):
        peer = lax.rem(me + d, total)
        pl.semaphore_signal(
            barrier, inc=1, device_id=(lax.div(peer, lon_n), lax.rem(peer, lon_n)), device_id_type=MESH
        )
        return carry

    lax.fori_loop(1, total, greet, 0)


def wait_all():
    lat_n, lon_n, lat_i, lon_i = place()
    pl.semaphore_wait(pltpu.get_barrier_semaphore(), lat_n * lon_n - 1)


def signal_near():
    lat_n, lon_n, lat_i, lon_i = place()
    barrier = pltpu.get_barrier_semaphore()
    for near in (lax.rem(lon_i + 1, lon_n), lax.rem(lon_i + lon_n - 1, lon_n)):
        pl.semaphore_signal(barrier, inc=1, device_id=(lat_i, near), device_id_type=MESH)

    @pl.when(lat_i > 0)
    def _():
        pl.semaphore_signal(barrier, inc=1, device_id=(lat_i - 1, lon_i), device_id_type=MESH)

    @pl.when(lat_i < lat_n - 1)
    def _():
        pl.semaphore_signal(barrier, inc=1, device_id=(lat_i + 1, lon_i), device_id_type=MESH)


def wait_near():
    lat_n, lon_n, lat_i, lon_i = place()
    peers = 2 + jnp.where(lat_i > 0, 1, 0) + jnp.where(lat_i < lat_n - 1, 1, 0)
    pl.semaphore_wait(pltpu.get_barrier_semaphore(), peers)


def trade_copy(sent, got, send_sems, recv_sems, peer, slot, lon_n):
    return pltpu.make_async_remote_copy(
        src_ref=sent.at[peer],
        dst_ref=got.at[slot],
        send_sem=send_sems.at[peer],
        recv_sem=recv_sems.at[slot],
        device_id=(lax.div(peer, lon_n), lax.rem(peer, lon_n)),
        device_id_type=MESH,
    )


def trade_start(sent, got, send_sems, recv_sems):
    lat_n, lon_n, lat_i, lon_i = place()
    total = lat_n * lon_n
    me = lat_i * lon_n + lon_i

    def send(d, carry):
        peer = lax.rem(me + d, total)
        trade_copy(sent, got, send_sems, recv_sems, peer, me, lon_n).start()
        return carry

    lax.fori_loop(1, total, send, 0)
    got[me] = sent[me]


def trade_wait(sent, got, send_sems, recv_sems):
    lat_n, lon_n, lat_i, lon_i = place()
    total = lat_n * lon_n
    me = lat_i * lon_n + lon_i

    def finish(d, carry):
        peer = lax.rem(me + d, total)
        copy = trade_copy(sent, got, send_sems, recv_sems, peer, peer, lon_n)
        copy.wait_send()
        copy.wait_recv()
        return carry

    lax.fori_loop(1, total, finish, 0)


def part(ref, rows, columns):
    if len(ref.shape) == 4:
        return ref.at[:, pl.ds(*rows), pl.ds(*columns)]
    return ref.at[pl.ds(*rows), pl.ds(*columns)]


def halo_copies(wide, send_sems, recv_sems):
    lat_n, lon_n, lat_i, lon_i = place()
    rows, columns = wide.shape[-3], wide.shape[-2]
    inner = (HLON, columns - 2 * HLON)

    def copy(index, source, target, device):
        return pltpu.make_async_remote_copy(
            src_ref=source,
            dst_ref=target,
            send_sem=send_sems.at[index],
            recv_sem=recv_sems.at[index],
            device_id=device,
            device_id_type=MESH,
        )

    down = copy(0, part(wide, (HROW, HROW), inner), part(wide, (rows - HROW, HROW), inner), (lat_i - 1, lon_i))
    up = copy(1, part(wide, (rows - 2 * HROW, HROW), inner), part(wide, (0, HROW), inner), (lat_i + 1, lon_i))
    west = copy(
        2,
        part(wide, (0, rows), (HLON, HLON)),
        part(wide, (0, rows), (columns - HLON, HLON)),
        (lat_i, lax.rem(lon_i + lon_n - 1, lon_n)),
    )
    east = copy(
        3,
        part(wide, (0, rows), (columns - 2 * HLON, HLON)),
        part(wide, (0, rows), (0, HLON)),
        (lat_i, lax.rem(lon_i + 1, lon_n)),
    )
    return down, up, west, east


def lat_edges(wide):
    lat_n, lon_n, lat_i, lon_i = place()
    rows = wide.shape[-3]
    for ends, first in ((lat_i == 0, 0), (lat_i == lat_n - 1, rows - HROW)):

        @pl.when(ends)
        def _(first=first):
            if len(wide.shape) == 4:
                for index in range(wide.shape[0]):
                    for row in range(HROW):
                        wide[index, first + row] = jnp.zeros(wide.shape[2:], jnp.float32)
            else:
                for row in range(HROW):
                    wide[first + row] = jnp.zeros(wide.shape[1:], jnp.float32)


def lat_start(down, up):
    lat_n, lon_n, lat_i, lon_i = place()

    @pl.when(lat_i > 0)
    def _():
        down.start()

    @pl.when(lat_i < lat_n - 1)
    def _():
        up.start()


def lat_wait(down, up):
    lat_n, lon_n, lat_i, lon_i = place()

    @pl.when(lat_i > 0)
    def _():
        down.wait_send()
        up.wait_recv()

    @pl.when(lat_i < lat_n - 1)
    def _():
        up.wait_send()
        down.wait_recv()


def dot(left, right, axes=((1,), (0,))):
    return lax.dot_general(
        left, right, (axes, ((), ())), precision=PRECISE, preferred_element_type=jnp.float32
    )


def full_sum(values):
    return jnp.sum(jnp.sum(values, axis=0, keepdims=True), axis=1, keepdims=True)


def gathered_sum(got, first, lane_index):
    tile = jnp.sum(got[:, :, first : first + LANES], axis=0)
    lane = lax.broadcasted_iota(jnp.int32, tile.shape, 1)
    row = lax.broadcasted_iota(jnp.int32, tile.shape, 0)
    return full_sum(jnp.where((lane == lane_index) & (row == 0), tile, 0.0))


def chooser(latitudes):
    rows = latitudes // FOOT
    row = lax.broadcasted_iota(jnp.int32, (latitudes, latitudes), 0)
    column = lax.broadcasted_iota(jnp.int32, (latitudes, latitudes), 1)
    return (column == lax.rem(row, rows) * FOOT + lax.div(row, rows)).astype(jnp.float32)


def regroup(pieces, levels):
    block = lax.div(lax.broadcasted_iota(jnp.int32, pieces[0][0].shape, 1), levels)
    grouped = []
    for i in range(FOOT):
        value = pieces[i][i]
        for q in range(FOOT):
            if q != i:
                moved = pltpu.roll(pieces[q][i], (q - i) % FOOT * levels, 1)
                value = jnp.where(block == q, moved, value)
        grouped.append(value)
    return grouped


def fold(natural, store):
    levels, columns, latitudes = natural.shape
    rows = latitudes // FOOT
    choose = chooser(latitudes)

    def group(index, carry):
        stack = jnp.concatenate([natural[:, FOOT * index + i, :] for i in range(FOOT)], axis=0)
        mixed = dot(choose, stack, ((1,), (1,)))
        pieces = [[mixed[q * rows : (q + 1) * rows]] * FOOT for q in range(FOOT)]
        for i, value in enumerate(regroup(pieces, levels)):
            store(FOOT * index + i, value)
        return carry

    lax.fori_loop(0, columns // FOOT, group, 0)


def unfold(folded, natural):
    levels, columns, latitudes = natural.shape
    choose = chooser(latitudes)

    def group(index, carry):
        planes = [folded[:, FOOT * index + i, :] for i in range(FOOT)]
        mixed = jnp.concatenate(regroup([[plane] * FOOT for plane in planes], levels), axis=0)
        stack = dot(mixed, choose, ((0,), (0,)))
        for i in range(FOOT):
            natural[:, FOOT * index + i, :] = stack[i * levels : (i + 1) * levels]
        return carry

    lax.fori_loop(0, columns // FOOT, group, 0)


def first_kernel(
    count, owner, spot, innovations, matrix, courant_lon, courant_lat, deviation,
    rows_out, anchors_out, permuted, residual, packing, norm_out, wide,
    sent, got, send_sems, recv_sems, halo_send, halo_recv,
):
    slots, block_total = packing.shape
    total = slots // DEPTH
    width = matrix.shape[0]
    lat_edges(wide)
    signal_all()
    live_column = lax.broadcasted_iota(jnp.int32, (block_total, 1), 0) < count[0]
    start = jnp.where(live_column, dot(innovations[...], matrix[...], ((1,), (1,))), 0.0)
    residual[...] = start
    row = lax.broadcasted_iota(jnp.int32, (width, width), 0)
    column = lax.broadcasted_iota(jnp.int32, (width, width), 1)
    footprint = FOOT * FOOT
    shuffle = column == lax.rem(row, footprint) * (width // footprint) + lax.div(row, footprint)
    shuffle = shuffle.astype(jnp.float32)
    weighted = dot(dot(start, matrix[...]), shuffle)

    live_row = lax.broadcasted_iota(jnp.int32, (1, block_total), 1) < count[0]
    owners = owner[...]
    tiles = lax.broadcasted_iota(jnp.int32, (total, block_total), 0)
    named = jnp.where((tiles == owners) & live_row, 1.0, 0.0)
    earlier = lax.broadcasted_iota(jnp.int32, (block_total, block_total), 0) < lax.broadcasted_iota(
        jnp.int32, (block_total, block_total), 1
    )
    ranks = jnp.sum(named * dot(named, earlier.astype(jnp.float32)), axis=0, keepdims=True)
    target = owners.astype(jnp.float32) * DEPTH + ranks
    slot_ids = lax.broadcasted_iota(jnp.int32, (slots, block_total), 0).astype(jnp.float32)
    pack = jnp.where((slot_ids == target) & live_row, 1.0, 0.0)
    packing[...] = pack
    sent[:, :, :width] = dot(pack, weighted).reshape(total, DEPTH, width)
    lane = lax.broadcasted_iota(jnp.int32, (slots, LANES), 1)
    spots = jnp.where(lane == 2, full_sum(start * start), dot(pack, spot[...]))
    sent[:, :, width:] = spots.reshape(total, DEPTH, LANES)
    wait_all()
    trade_start(sent, got, send_sems, recv_sems)
    for index, natural in enumerate((courant_lon, courant_lat, deviation)):

        def store(place_in, value, index=index):
            wide[index, pl.ds(HROW, value.shape[0]), HLON + place_in, :] = value

        fold(natural, store)
    down, up, west, east = halo_copies(wide, halo_send, halo_recv)
    lat_start(down, up)
    permuted[...] = dot(matrix[...], shuffle)
    lat_wait(down, up)
    west.start()
    east.start()
    trade_wait(sent, got, send_sems, recv_sems)
    unload(got, rows_out)
    anchors_out[...] = got[:, :, width:].reshape(slots, LANES)
    norm_out[...] = jnp.broadcast_to(gathered_sum(got, width, 2), norm_out.shape)
    west.wait()
    east.wait()


def unload(got, rows_out):
    slots, groups = rows_out.shape[:2]
    for group in range(groups):
        rows_out[:, group, :] = got[:, :, group * LANES : (group + 1) * LANES].reshape(slots, LANES)


def spread_kernel(anchors, rows, field):
    slots = rows.shape[0]
    level_lanes = LANES // FOOT
    field[...] = jnp.zeros(field.shape, jnp.float32)

    def add(slot, carry):
        column, latitude = anchors[slot], anchors[slots + slot]
        row, shift = lax.div(latitude, FOOT), lax.rem(latitude, FOOT) * level_lanes
        patch = pltpu.roll(rows[slot], shift, 1)
        lane = lax.broadcasted_iota(jnp.int32, patch.shape, 1)
        here = lane >= shift
        field[row, pl.ds(column, FOOT), :] += jnp.where(here, patch, 0.0)
        field[row + 1, pl.ds(column, FOOT), :] += jnp.where(here, 0.0, patch)
        return carry

    lax.fori_loop(0, slots, add, 0, unroll=8)


def sample_kernel(anchors, field, rows):
    slots = rows.shape[0]
    level_lanes = LANES // FOOT

    def pick(slot, carry):
        column, latitude = anchors[slot], anchors[slots + slot]
        row, shift = lax.div(latitude, FOOT), lax.rem(latitude, FOOT) * level_lanes
        here = field[row, pl.ds(column, FOOT), :]
        after = field[row + 1, pl.ds(column, FOOT), :]
        lane = lax.broadcasted_iota(jnp.int32, here.shape, 1)
        rows[slot] = pltpu.roll(jnp.where(lane >= shift, here, after), lax.rem(LANES - shift, LANES), 1)
        return carry

    lax.fori_loop(0, slots, pick, 0, unroll=8)


def model_step(now, later, wide, adjoint):
    lat_n, lon_n, lat_i, lon_i = place()
    rows, columns = now.shape[0], now.shape[1]
    level_lanes = LANES // FOOT
    low = jnp.where(lat_i > 0, 1.0, 0.0)
    high = jnp.where(lat_i < lat_n - 1, 1.0, 0.0)
    lane = lax.broadcasted_iota(jnp.int32, (columns, LANES), 1)
    first, last = lane < level_lanes, lane >= LANES - level_lanes

    def plane(row, carry):
        before, after = lax.rem(row + rows - 1, rows), lax.rem(row + 1, rows)
        here = now[row]
        prior = jnp.where(last, now[before], here)
        following = jnp.where(first, now[after], here)
        zonal, meridional = 0.5 * wide[0, row], wide[1, row]
        if adjoint:
            prior_wind = jnp.where(last, wide[1, before], meridional)
            next_wind = jnp.where(first, wide[1, after], meridional)
            value = (
                CENTRE * here
                + pltpu.roll((DIFFUSION - zonal) * here, 1, 0)
                + pltpu.roll((DIFFUSION + zonal) * here, columns - 1, 0)
                + pltpu.roll((DIFFUSION - 0.5 * prior_wind) * prior, level_lanes, 1)
                + pltpu.roll((DIFFUSION + 0.5 * next_wind) * following, LANES - level_lanes, 1)
            )
        else:
            value = (
                CENTRE * here
                + (DIFFUSION - zonal) * pltpu.roll(here, columns - 1, 0)
                + (DIFFUSION + zonal) * pltpu.roll(here, 1, 0)
                + (DIFFUSION - 0.5 * meridional) * pltpu.roll(following, LANES - level_lanes, 1)
                + (DIFFUSION + 0.5 * meridional) * pltpu.roll(prior, level_lanes, 1)
            )
        keep = jnp.where(row < HROW, low, jnp.where(row >= rows - HROW, high, 1.0))
        later[row] = value * keep
        return carry

    lax.fori_loop(0, rows, plane, 0, unroll=4)


def model_steps(held, other, wide, adjoint):
    def pair(index, carry):
        model_step(held, other, wide, adjoint)
        model_step(other, held, wide, adjoint)
        return carry

    lax.fori_loop(0, STEPS // 2, pair, 0)


def load_wide(field, held, send_sems, recv_sems, signal, wait):
    columns = field.shape[1]
    lat_edges(held)
    signal()

    def fill(row, carry):
        held[HROW + row, pl.ds(HLON, columns)] = field[row]
        return carry

    lax.fori_loop(0, held.shape[0] - 2 * HROW, fill, 0)
    down, up, west, east = halo_copies(held, send_sems, recv_sems)
    wait()
    lat_start(down, up)
    lat_wait(down, up)
    west.start()
    east.start()
    west.wait()
    east.wait()


def system_kernel(field, wide, adjoint_out, scaled_out, forward_out, energy_out, held, other, send_sems, recv_sems):
    rows, columns = held.shape[0], held.shape[1]
    own = columns - 2 * HLON
    load_wide(field, held, send_sems, recv_sems, signal_near, wait_near)
    model_steps(held, other, wide, True)

    def scale(row, energy):
        value, deviation = held[row], wide[2, row]
        scaled = deviation * deviation * value
        held[row] = scaled
        adjoint_out[row - HROW] = value[HLON : HLON + own]
        scaled_out[row - HROW] = scaled[HLON : HLON + own]
        return energy + (scaled * value)[HLON : HLON + own]

    energy = lax.fori_loop(HROW, rows - HROW, scale, jnp.zeros((own, LANES), jnp.float32))
    energy_out[...] = jnp.broadcast_to(full_sum(energy), energy_out.shape)
    for row in (*range(HROW), *range(rows - HROW, rows)):
        deviation = wide[2, row]
        held[row] = deviation * deviation * held[row]
    model_steps(held, other, wide, False)

    def write(row, carry):
        forward_out[row] = held[HROW + row, pl.ds(HLON, own)]
        return carry

    lax.fori_loop(0, rows - 2 * HROW, write, 0)
    forward_out[rows - 2 * HROW] = jnp.zeros((own, LANES), jnp.float32)


def return_kernel(
    rows, energy, matrix, start, packing, norm, scaled,
    rows_out, natural_out, direction, step_out, ratio_out, norm_out, square_out,
    sent, got, sent_next, got_next, send_sems, recv_sems, send_next, recv_next,
):
    slots, groups = rows.shape[:2]
    total = slots // DEPTH
    width = matrix.shape[0]
    signal_all()
    for group in range(groups):
        sent[:, :, group * LANES : (group + 1) * LANES] = rows[:, group, :].reshape(total, DEPTH, LANES)
    sent[:, :, width:] = jnp.broadcast_to(energy[...][None], (total, DEPTH, LANES))
    wait_all()
    trade_start(sent, got, send_sems, recv_sems)
    unfold(scaled, natural_out)
    trade_wait(sent, got, send_sems, recv_sems)
    norm_first = norm[0:1, 0:1]
    step = norm_first / (norm_first + gathered_sum(got, width, 0))
    back = dot(packing[...], got[:, :, :width].reshape(slots, width), ((0,), (0,)))
    image = start[...] + dot(back, matrix[...], ((1,), (1,)))
    residual = start[...] - step * image
    pack = packing[...]
    sent_next[:, :, :width] = dot(pack, dot(residual, matrix[...])).reshape(total, DEPTH, width)
    sent_next[:, :, width:] = jnp.broadcast_to(full_sum(residual * residual)[None], (total, DEPTH, LANES))
    trade_start(sent_next, got_next, send_next, recv_next)
    trade_wait(sent_next, got_next, send_next, recv_next)
    unload(got_next, rows_out)
    norm_next = gathered_sum(got_next, width, 0)
    ratio = norm_next / norm_first
    moved = residual + ratio * start[...]
    direction[...] = moved
    step_out[...] = jnp.broadcast_to(step, step_out.shape)
    ratio_out[...] = jnp.broadcast_to(ratio, ratio_out.shape)
    norm_out[...] = jnp.broadcast_to(norm_next, norm_out.shape)
    square_out[...] = jnp.broadcast_to(full_sum(moved * moved), square_out.shape)


def last_kernel(
    field, wide, earlier, ratio, norm, square,
    natural_out, step_out,
    held, other, scaled, sent, got, halo_send, halo_recv, send_sems, recv_sems,
):
    rows, columns = held.shape[0], held.shape[1]
    own = columns - 2 * HLON
    load_wide(field, held, halo_send, halo_recv, signal_all, wait_all)
    model_steps(held, other, wide, True)
    scale = ratio[0:1, 0:1]

    def combine(row, energy):
        value = held[HROW + row, pl.ds(HLON, own)] + scale * earlier[row]
        deviation = wide[2, HROW + row, pl.ds(HLON, own)]
        product = deviation * deviation * value
        scaled[row] = product
        return energy + product * value

    energy = lax.fori_loop(0, rows - 2 * HROW, combine, jnp.zeros((own, LANES), jnp.float32))
    sent[...] = jnp.broadcast_to((full_sum(energy) + square[0:1, 0:1])[None], sent.shape)
    trade_start(sent, got, send_sems, recv_sems)
    unfold(scaled, natural_out)
    trade_wait(sent, got, send_sems, recv_sems)
    step_out[...] = jnp.broadcast_to(norm[0:1, 0:1] / gathered_sum(got, 0, 0), step_out.shape)


def vmem(count):
    return [pl.BlockSpec(memory_space=pltpu.VMEM)] * count


def smem():
    return pl.BlockSpec(memory_space=pltpu.SMEM)


def shape(*sizes):
    return jax.ShapeDtypeStruct(sizes, jnp.float32)


def params(collective_id=None):
    if collective_id is None:
        return pltpu.CompilerParams(vmem_limit_bytes=LIMIT)
    return pltpu.CompilerParams(
        collective_id=collective_id, has_side_effects=True, vmem_limit_bytes=LIMIT
    )


def body(
    innovations, block_owner, block_lat, block_lon, block_count,
    error_weight, courant_lon, courant_lat, background_std,
):
    total = lax.axis_size("lat") * lax.axis_size("lon")
    block_total, width = innovations.shape
    levels, columns, latitudes = courant_lon.shape
    rows = latitudes // FOOT
    slots = total * DEPTH
    groups = width // LANES
    wide_rows, wide_columns = rows + 2 * HROW, columns + 2 * HLON
    spot = jnp.pad(
        jnp.stack([block_lon, block_lat], axis=1).astype(jnp.float32), ((0, 0), (0, LANES - 2))
    )
    tile = shape(DEPTH, LANES)
    chunks = pltpu.VMEM((total, DEPTH, width + LANES), jnp.float32)
    dma = pltpu.SemaphoreType.DMA

    arrived, anchors, matrix, start, packing, norm, wide = pl.pallas_call(
        first_kernel,
        out_shape=(
            shape(slots, groups, LANES), shape(slots, LANES), shape(width, width),
            shape(block_total, width), shape(slots, block_total), tile,
            shape(3, wide_rows, wide_columns, LANES),
        ),
        in_specs=[smem()] + vmem(7),
        out_specs=tuple(vmem(7)),
        scratch_shapes=[chunks, chunks, dma((total,)), dma((total,)), dma((4,)), dma((4,))],
        compiler_params=params(0),
    )(block_count, block_owner.reshape(1, block_total), spot, innovations, error_weight[0], courant_lon, courant_lat, background_std)

    corners = jnp.concatenate([anchors[:, 0], anchors[:, 1]]).astype(jnp.int32)

    def spread(block_rows):
        return pl.pallas_call(
            spread_kernel,
            out_shape=shape(rows + 1, columns, LANES),
            in_specs=[smem()] + vmem(1),
            out_specs=vmem(1)[0],
            compiler_params=params(),
        )(corners, block_rows)

    held = pltpu.VMEM((wide_rows, wide_columns, LANES), jnp.float32)
    first, scaled, model_state, energy = pl.pallas_call(
        system_kernel,
        out_shape=(shape(rows, columns, LANES), shape(rows, columns, LANES), shape(rows + 1, columns, LANES), tile),
        in_specs=vmem(2),
        out_specs=tuple(vmem(4)),
        scratch_shapes=[held, held, dma((4,)), dma((4,))],
        compiler_params=params(1),
    )(spread(arrived), wide)

    picked = pl.pallas_call(
        sample_kernel,
        out_shape=shape(slots, groups, LANES),
        in_specs=[smem()] + vmem(1),
        out_specs=vmem(1)[0],
        compiler_params=params(),
    )(corners, model_state)

    arrived, first_part, direction, step_first, ratio, norm_next, square = pl.pallas_call(
        return_kernel,
        out_shape=(
            shape(slots, groups, LANES), shape(levels, columns, latitudes), shape(block_total, width),
            tile, tile, tile, tile,
        ),
        in_specs=vmem(7),
        out_specs=tuple(vmem(7)),
        scratch_shapes=[chunks, chunks, chunks, chunks] + [dma((total,))] * 4,
        compiler_params=params(2),
    )(picked, energy, matrix, start, packing, norm, scaled)

    tiles = pltpu.VMEM((total, DEPTH, LANES), jnp.float32)
    second_part, step_second = pl.pallas_call(
        last_kernel,
        out_shape=(shape(levels, columns, latitudes), tile),
        in_specs=vmem(6),
        out_specs=tuple(vmem(2)),
        scratch_shapes=[held, held, pltpu.VMEM((rows, columns, LANES), jnp.float32), tiles, tiles, dma((4,)), dma((4,)), dma((total,)), dma((total,))],
        compiler_params=params(3),
    )(spread(arrived), wide, first, ratio, norm_next, square)

    step_first, step_second = step_first[0, 0], step_second[0, 0]
    solution = step_first * start + step_second * direction
    return solution, step_first * first_part + step_second * second_part


def solution(mesh):
    blocks = P(("lat", "lon"))
    in_specs = (
        P(("lat", "lon"), None),
        P(("lat", "lon"), None),
        blocks,
        blocks,
        blocks,
        P(("lat", "lon"), None, None),
        P(None, "lon", "lat"),
        P(None, "lon", "lat"),
        P(None, "lon", "lat"),
    )
    out_specs = (P(("lat", "lon"), None), P(None, "lon", "lat"))
    return jax.shard_map(body, mesh=mesh, in_specs=in_specs, out_specs=out_specs, check_vma=False)
```

```python
import functools

import jax
import jax.numpy as jnp
from jax import lax
from jax.experimental import pallas as pl
from jax.experimental.pallas import tpu as pltpu
from jax.sharding import PartitionSpec as P

FOOT = 4
STEPS = 4
DIFFUSION = 0.15
CENTRE = 1.0 - 4.0 * DIFFUSION
PRECISE = lax.Precision.HIGHEST
MESH = pl.DeviceIdType.MESH
LANES = 128
DEPTH = 8
HLON = 8
HROW = 2
LIMIT = 48 * 1024 * 1024


def place():
    lat_n, lon_n = lax.axis_size("lat"), lax.axis_size("lon")
    lat_i, lon_i = lax.axis_index("lat"), lax.axis_index("lon")
    return lat_n, lon_n, lat_i, lon_i


def signal_all():
    lat_n, lon_n, lat_i, lon_i = place()
    total = lat_n * lon_n
    me = lat_i * lon_n + lon_i
    barrier = pltpu.get_barrier_semaphore()

    def greet(d, carry):
        peer = lax.rem(me + d, total)
        pl.semaphore_signal(
            barrier, inc=1, device_id=(lax.div(peer, lon_n), lax.rem(peer, lon_n)), device_id_type=MESH
        )
        return carry

    lax.fori_loop(1, total, greet, 0)


def wait_all():
    lat_n, lon_n, lat_i, lon_i = place()
    pl.semaphore_wait(pltpu.get_barrier_semaphore(), lat_n * lon_n - 1)


def signal_near():
    lat_n, lon_n, lat_i, lon_i = place()
    barrier = pltpu.get_barrier_semaphore()
    for near in (lax.rem(lon_i + 1, lon_n), lax.rem(lon_i + lon_n - 1, lon_n)):
        pl.semaphore_signal(barrier, inc=1, device_id=(lat_i, near), device_id_type=MESH)

    @pl.when(lat_i > 0)
    def _():
        pl.semaphore_signal(barrier, inc=1, device_id=(lat_i - 1, lon_i), device_id_type=MESH)

    @pl.when(lat_i < lat_n - 1)
    def _():
        pl.semaphore_signal(barrier, inc=1, device_id=(lat_i + 1, lon_i), device_id_type=MESH)


def wait_near():
    lat_n, lon_n, lat_i, lon_i = place()
    peers = 2 + jnp.where(lat_i > 0, 1, 0) + jnp.where(lat_i < lat_n - 1, 1, 0)
    pl.semaphore_wait(pltpu.get_barrier_semaphore(), peers)


def trade_copy(sent, got, send_sems, recv_sems, peer, slot, lon_n):
    return pltpu.make_async_remote_copy(
        src_ref=sent.at[peer],
        dst_ref=got.at[slot],
        send_sem=send_sems.at[peer],
        recv_sem=recv_sems.at[slot],
        device_id=(lax.div(peer, lon_n), lax.rem(peer, lon_n)),
        device_id_type=MESH,
    )


def trade_start(sent, got, send_sems, recv_sems):
    lat_n, lon_n, lat_i, lon_i = place()
    total = lat_n * lon_n
    me = lat_i * lon_n + lon_i

    def send(d, carry):
        peer = lax.rem(me + d, total)
        trade_copy(sent, got, send_sems, recv_sems, peer, me, lon_n).start()
        return carry

    lax.fori_loop(1, total, send, 0)
    got[me] = sent[me]


def trade_wait(sent, got, send_sems, recv_sems):
    lat_n, lon_n, lat_i, lon_i = place()
    total = lat_n * lon_n
    me = lat_i * lon_n + lon_i

    def finish(d, carry):
        peer = lax.rem(me + d, total)
        copy = trade_copy(sent, got, send_sems, recv_sems, peer, peer, lon_n)
        copy.wait_send()
        copy.wait_recv()
        return carry

    lax.fori_loop(1, total, finish, 0)


def part(ref, rows, columns):
    if len(ref.shape) == 4:
        return ref.at[:, pl.ds(*rows), pl.ds(*columns)]
    return ref.at[pl.ds(*rows), pl.ds(*columns)]


def halo_copies(wide, send_sems, recv_sems):
    lat_n, lon_n, lat_i, lon_i = place()
    rows, columns = wide.shape[-3], wide.shape[-2]
    inner = (HLON, columns - 2 * HLON)

    def copy(index, source, target, device):
        return pltpu.make_async_remote_copy(
            src_ref=source,
            dst_ref=target,
            send_sem=send_sems.at[index],
            recv_sem=recv_sems.at[index],
            device_id=device,
            device_id_type=MESH,
        )

    down = copy(0, part(wide, (HROW, HROW), inner), part(wide, (rows - HROW, HROW), inner), (lat_i - 1, lon_i))
    up = copy(1, part(wide, (rows - 2 * HROW, HROW), inner), part(wide, (0, HROW), inner), (lat_i + 1, lon_i))
    west = copy(
        2,
        part(wide, (0, rows), (HLON, HLON)),
        part(wide, (0, rows), (columns - HLON, HLON)),
        (lat_i, lax.rem(lon_i + lon_n - 1, lon_n)),
    )
    east = copy(
        3,
        part(wide, (0, rows), (columns - 2 * HLON, HLON)),
        part(wide, (0, rows), (0, HLON)),
        (lat_i, lax.rem(lon_i + 1, lon_n)),
    )
    return down, up, west, east


def lat_edges(wide):
    lat_n, lon_n, lat_i, lon_i = place()
    rows = wide.shape[-3]
    for ends, first in ((lat_i == 0, 0), (lat_i == lat_n - 1, rows - HROW)):

        @pl.when(ends)
        def _(first=first):
            if len(wide.shape) == 4:
                for index in range(wide.shape[0]):
                    for row in range(HROW):
                        wide[index, first + row] = jnp.zeros(wide.shape[2:], jnp.float32)
            else:
                for row in range(HROW):
                    wide[first + row] = jnp.zeros(wide.shape[1:], jnp.float32)


def lat_start(down, up):
    lat_n, lon_n, lat_i, lon_i = place()

    @pl.when(lat_i > 0)
    def _():
        down.start()

    @pl.when(lat_i < lat_n - 1)
    def _():
        up.start()


def lat_wait(down, up):
    lat_n, lon_n, lat_i, lon_i = place()

    @pl.when(lat_i > 0)
    def _():
        down.wait_send()
        up.wait_recv()

    @pl.when(lat_i < lat_n - 1)
    def _():
        up.wait_send()
        down.wait_recv()


def dot(left, right, axes=((1,), (0,))):
    return lax.dot_general(
        left, right, (axes, ((), ())), precision=PRECISE, preferred_element_type=jnp.float32
    )


def full_sum(values):
    return jnp.sum(jnp.sum(values, axis=0, keepdims=True), axis=1, keepdims=True)


def gathered_sum(got, lane_index):
    tile = jnp.sum(got[...], axis=0)
    lane = lax.broadcasted_iota(jnp.int32, tile.shape, 1)
    row = lax.broadcasted_iota(jnp.int32, tile.shape, 0)
    return full_sum(jnp.where((lane == lane_index) & (row == 0), tile, 0.0))


def chooser(latitudes):
    rows = latitudes // FOOT
    row = lax.broadcasted_iota(jnp.int32, (latitudes, latitudes), 0)
    column = lax.broadcasted_iota(jnp.int32, (latitudes, latitudes), 1)
    return (column == lax.rem(row, rows) * FOOT + lax.div(row, rows)).astype(jnp.float32)


def regroup(pieces, levels):
    block = lax.div(lax.broadcasted_iota(jnp.int32, pieces[0][0].shape, 1), levels)
    grouped = []
    for i in range(FOOT):
        value = pieces[i][i]
        for q in range(FOOT):
            if q != i:
                moved = pltpu.roll(pieces[q][i], (q - i) % FOOT * levels, 1)
                value = jnp.where(block == q, moved, value)
        grouped.append(value)
    return grouped


def fold(fields, store):
    count, levels, columns, latitudes = fields.shape
    rows = latitudes // FOOT
    choose = chooser(latitudes)

    def group(index, carry):
        for field in range(count):
            stack = jnp.concatenate([fields[field, :, FOOT * index + i, :] for i in range(FOOT)], axis=0)
            mixed = dot(choose, stack, ((1,), (1,)))
            pieces = [[mixed[q * rows : (q + 1) * rows]] * FOOT for q in range(FOOT)]
            for i, value in enumerate(regroup(pieces, levels)):
                store(field, FOOT * index + i, value)
        return carry

    lax.fori_loop(0, columns // FOOT, group, 0, unroll=2)


def unfold(folded, natural):
    levels, columns, latitudes = natural.shape
    choose = chooser(latitudes)

    def group(index, carry):
        planes = [folded[:, FOOT * index + i, :] for i in range(FOOT)]
        mixed = jnp.concatenate(regroup([[plane] * FOOT for plane in planes], levels), axis=0)
        stack = dot(mixed, choose, ((0,), (0,)))
        for i in range(FOOT):
            natural[:, FOOT * index + i, :] = stack[i * levels : (i + 1) * levels]
        return carry

    lax.fori_loop(0, columns // FOOT, group, 0, unroll=5)


def first_kernel(
    count, owner, spot, innovations, matrix, courant_lon, courant_lat, deviation,
    rows_out, anchors_out, permuted, residual, packing, norm_out, wide,
    sent, got, note, got_note, held_matrix, held_fields,
    send_sems, recv_sems, note_send, note_recv, halo_send, halo_recv, load_sems,
):
    slots, block_total = packing.shape
    total = slots // DEPTH
    width = matrix.shape[0]
    matrix_copy = pltpu.make_async_copy(matrix, held_matrix, load_sems.at[3])
    matrix_copy.start()
    field_copies = [
        pltpu.make_async_copy(natural, held_fields.at[index], load_sems.at[index])
        for index, natural in enumerate((courant_lon, courant_lat, deviation))
    ]
    for copy in field_copies:
        copy.start()
    lat_edges(wide)
    signal_all()
    matrix_copy.wait()
    live_column = lax.broadcasted_iota(jnp.int32, (block_total, 1), 0) < count[0]
    start = jnp.where(live_column, dot(innovations[...], held_matrix[...], ((1,), (1,))), 0.0)
    residual[...] = start
    row = lax.broadcasted_iota(jnp.int32, (width, width), 0)
    column = lax.broadcasted_iota(jnp.int32, (width, width), 1)
    footprint = FOOT * FOOT
    shuffle = column == lax.rem(row, footprint) * (width // footprint) + lax.div(row, footprint)
    shuffle = shuffle.astype(jnp.float32)
    weighted = dot(dot(start, held_matrix[...]), shuffle)

    live_row = lax.broadcasted_iota(jnp.int32, (1, block_total), 1) < count[0]
    owners = owner[...]
    tiles = lax.broadcasted_iota(jnp.int32, (total, block_total), 0)
    named = jnp.where((tiles == owners) & live_row, 1.0, 0.0)
    earlier = lax.broadcasted_iota(jnp.int32, (block_total, block_total), 0) < lax.broadcasted_iota(
        jnp.int32, (block_total, block_total), 1
    )
    ranks = jnp.sum(named * dot(named, earlier.astype(jnp.float32)), axis=0, keepdims=True)
    target = owners.astype(jnp.float32) * DEPTH + ranks
    slot_ids = lax.broadcasted_iota(jnp.int32, (slots, block_total), 0).astype(jnp.float32)
    pack = jnp.where((slot_ids == target) & live_row, 1.0, 0.0)
    packing[...] = pack
    sent[...] = dot(pack, weighted).reshape(total, DEPTH, width)
    spots = dot(pack, spot[...]).reshape(total, DEPTH, LANES)
    lane = lax.broadcasted_iota(jnp.int32, spots.shape, 2)
    depth = lax.broadcasted_iota(jnp.int32, spots.shape, 1)
    spots = jnp.sum(jnp.where(lax.rem(lane, DEPTH) == depth, spots, 0.0), axis=1, keepdims=True)
    lane = lax.broadcasted_iota(jnp.int32, spots.shape, 2)
    note[...] = jnp.where(lane == 2 * DEPTH, full_sum(start * start)[None], spots)
    wait_all()
    trade_start(sent, got, send_sems, recv_sems)
    trade_start(note, got_note, note_send, note_recv)
    for copy in field_copies:
        copy.wait()

    def store(index, column, value):
        wide[index, pl.ds(HROW, value.shape[0]), HLON + column, :] = value

    fold(held_fields, store)
    down, up, west, east = halo_copies(wide, halo_send, halo_recv)
    lat_start(down, up)
    permuted[...] = dot(held_matrix[...], shuffle)
    lat_wait(down, up)
    west.start()
    east.start()
    trade_wait(sent, got, send_sems, recv_sems)
    trade_wait(note, got_note, note_send, note_recv)
    unload(got, rows_out)
    anchors_out[...] = got_note[...].reshape(total, LANES)
    norm_out[...] = jnp.broadcast_to(gathered_sum(got_note, 2 * DEPTH), norm_out.shape)
    west.wait()
    east.wait()


def unload(got, rows_out):
    slots, groups = rows_out.shape[:2]
    for group in range(groups):
        rows_out[:, group, :] = got[:, :, group * LANES : (group + 1) * LANES].reshape(slots, LANES)


def spread_kernel(anchors, rows, field):
    slots = rows.shape[0]
    level_lanes = LANES // FOOT
    field[...] = jnp.zeros(field.shape, jnp.float32)

    def add(slot, carry):
        column, latitude = anchors[slot], anchors[slots + slot]
        row, shift = lax.div(latitude, FOOT), lax.rem(latitude, FOOT) * level_lanes
        patch = pltpu.roll(rows[slot], shift, 1)
        lane = lax.broadcasted_iota(jnp.int32, patch.shape, 1)
        here = lane >= shift
        field[row, pl.ds(column, FOOT), :] += jnp.where(here, patch, 0.0)
        field[row + 1, pl.ds(column, FOOT), :] += jnp.where(here, 0.0, patch)
        return carry

    lax.fori_loop(0, slots, add, 0, unroll=16)


def sample_kernel(anchors, field, rows):
    slots = rows.shape[0]
    level_lanes = LANES // FOOT

    def pick(slot, carry):
        column, latitude = anchors[slot], anchors[slots + slot]
        row, shift = lax.div(latitude, FOOT), lax.rem(latitude, FOOT) * level_lanes
        here = field[row, pl.ds(column, FOOT), :]
        after = field[row + 1, pl.ds(column, FOOT), :]
        lane = lax.broadcasted_iota(jnp.int32, here.shape, 1)
        rows[slot] = pltpu.roll(jnp.where(lane >= shift, here, after), lax.rem(LANES - shift, LANES), 1)
        return carry

    lax.fori_loop(0, slots, pick, 0, unroll=16)


def model_step(now, later, wide, adjoint):
    lat_n, lon_n, lat_i, lon_i = place()
    rows, columns = now.shape[0], now.shape[1]
    level_lanes = LANES // FOOT
    low = jnp.where(lat_i > 0, 1.0, 0.0)
    high = jnp.where(lat_i < lat_n - 1, 1.0, 0.0)
    lane = lax.broadcasted_iota(jnp.int32, (columns, LANES), 1)
    first, last = lane < level_lanes, lane >= LANES - level_lanes

    def plane(row, carry):
        before, after = lax.rem(row + rows - 1, rows), lax.rem(row + 1, rows)
        here = now[row]
        prior = jnp.where(last, now[before], here)
        following = jnp.where(first, now[after], here)
        zonal, meridional = 0.5 * wide[0, row], wide[1, row]
        if adjoint:
            prior_wind = jnp.where(last, wide[1, before], meridional)
            next_wind = jnp.where(first, wide[1, after], meridional)
            value = (
                CENTRE * here
                + pltpu.roll((DIFFUSION - zonal) * here, 1, 0)
                + pltpu.roll((DIFFUSION + zonal) * here, columns - 1, 0)
                + pltpu.roll((DIFFUSION - 0.5 * prior_wind) * prior, level_lanes, 1)
                + pltpu.roll((DIFFUSION + 0.5 * next_wind) * following, LANES - level_lanes, 1)
            )
        else:
            value = (
                CENTRE * here
                + (DIFFUSION - zonal) * pltpu.roll(here, columns - 1, 0)
                + (DIFFUSION + zonal) * pltpu.roll(here, 1, 0)
                + (DIFFUSION - 0.5 * meridional) * pltpu.roll(following, LANES - level_lanes, 1)
                + (DIFFUSION + 0.5 * meridional) * pltpu.roll(prior, level_lanes, 1)
            )
        keep = jnp.where(row < HROW, low, jnp.where(row >= rows - HROW, high, 1.0))
        later[row] = value * keep
        return carry

    lax.fori_loop(0, rows, plane, 0, unroll=4)


def model_steps(held, other, wide, adjoint):
    def pair(index, carry):
        model_step(held, other, wide, adjoint)
        model_step(other, held, wide, adjoint)
        return carry

    lax.fori_loop(0, STEPS // 2, pair, 0)


def load_wide(field, held, send_sems, recv_sems, signal, wait):
    columns = field.shape[1]
    lat_edges(held)
    signal()

    def fill(row, carry):
        held[HROW + row, pl.ds(HLON, columns)] = field[row]
        return carry

    lax.fori_loop(0, held.shape[0] - 2 * HROW, fill, 0)
    down, up, west, east = halo_copies(held, send_sems, recv_sems)
    wait()
    lat_start(down, up)
    lat_wait(down, up)
    west.start()
    east.start()
    west.wait()
    east.wait()


def system_kernel(field, wide, adjoint_out, scaled_out, forward_out, energy_out, held, other, send_sems, recv_sems):
    rows, columns = held.shape[0], held.shape[1]
    own = columns - 2 * HLON
    load_wide(field, held, send_sems, recv_sems, signal_near, wait_near)
    model_steps(held, other, wide, True)

    def scale(row, energy):
        value, deviation = held[row], wide[2, row]
        scaled = deviation * deviation * value
        held[row] = scaled
        adjoint_out[row - HROW] = value[HLON : HLON + own]
        scaled_out[row - HROW] = scaled[HLON : HLON + own]
        return energy + (scaled * value)[HLON : HLON + own]

    energy = lax.fori_loop(HROW, rows - HROW, scale, jnp.zeros((own, LANES), jnp.float32))
    energy_out[...] = jnp.broadcast_to(full_sum(energy), energy_out.shape)
    for row in (*range(HROW), *range(rows - HROW, rows)):
        deviation = wide[2, row]
        held[row] = deviation * deviation * held[row]
    model_steps(held, other, wide, False)

    def write(row, carry):
        forward_out[row] = held[HROW + row, pl.ds(HLON, own)]
        return carry

    lax.fori_loop(0, rows - 2 * HROW, write, 0)
    forward_out[rows - 2 * HROW] = jnp.zeros((own, LANES), jnp.float32)


def return_kernel(
    rows, energy, matrix, start, packing, norm, scaled,
    rows_out, natural_out, direction, step_out, ratio_out, norm_out, square_out,
    sent, got, sent_next, got_next, note, got_note, note_next, got_note_next,
    send_sems, recv_sems, send_next, recv_next, note_send, note_recv, note_send_next, note_recv_next,
):
    slots, groups = rows.shape[:2]
    total = slots // DEPTH
    width = matrix.shape[0]
    signal_all()
    for group in range(groups):
        sent[:, :, group * LANES : (group + 1) * LANES] = rows[:, group, :].reshape(total, DEPTH, LANES)
    note[...] = jnp.broadcast_to(energy[0:1][None], note.shape)
    wait_all()
    trade_start(sent, got, send_sems, recv_sems)
    trade_start(note, got_note, note_send, note_recv)
    unfold(scaled, natural_out)
    trade_wait(sent, got, send_sems, recv_sems)
    trade_wait(note, got_note, note_send, note_recv)
    norm_first = norm[0:1, 0:1]
    step = norm_first / (norm_first + gathered_sum(got_note, 0))
    back = dot(packing[...], got[...].reshape(slots, width), ((0,), (0,)))
    image = start[...] + dot(back, matrix[...], ((1,), (1,)))
    residual = start[...] - step * image
    pack = packing[...]
    sent_next[...] = dot(pack, dot(residual, matrix[...])).reshape(total, DEPTH, width)
    note_next[...] = jnp.broadcast_to(full_sum(residual * residual)[None], note_next.shape)
    trade_start(sent_next, got_next, send_next, recv_next)
    trade_start(note_next, got_note_next, note_send_next, note_recv_next)
    trade_wait(sent_next, got_next, send_next, recv_next)
    trade_wait(note_next, got_note_next, note_send_next, note_recv_next)
    unload(got_next, rows_out)
    norm_next = gathered_sum(got_note_next, 0)
    ratio = norm_next / norm_first
    moved = residual + ratio * start[...]
    direction[...] = moved
    step_out[...] = jnp.broadcast_to(step, step_out.shape)
    ratio_out[...] = jnp.broadcast_to(ratio, ratio_out.shape)
    norm_out[...] = jnp.broadcast_to(norm_next, norm_out.shape)
    square_out[...] = jnp.broadcast_to(full_sum(moved * moved), square_out.shape)


def last_kernel(
    field, wide, earlier, ratio, norm, square,
    natural_out, step_out,
    held, other, scaled, sent, got, halo_send, halo_recv, send_sems, recv_sems,
):
    rows, columns = held.shape[0], held.shape[1]
    own = columns - 2 * HLON
    load_wide(field, held, halo_send, halo_recv, signal_all, wait_all)
    model_steps(held, other, wide, True)
    scale = ratio[0:1, 0:1]

    def combine(row, energy):
        value = held[HROW + row, pl.ds(HLON, own)] + scale * earlier[row]
        deviation = wide[2, HROW + row, pl.ds(HLON, own)]
        product = deviation * deviation * value
        scaled[row] = product
        return energy + product * value

    energy = lax.fori_loop(0, rows - 2 * HROW, combine, jnp.zeros((own, LANES), jnp.float32))
    sent[...] = jnp.broadcast_to((full_sum(energy) + square[0:1, 0:1])[None], sent.shape)
    trade_start(sent, got, send_sems, recv_sems)
    unfold(scaled, natural_out)
    trade_wait(sent, got, send_sems, recv_sems)
    step_out[...] = jnp.broadcast_to(norm[0:1, 0:1] / gathered_sum(got, 0), step_out.shape)


def vmem(count):
    return [pl.BlockSpec(memory_space=pltpu.VMEM)] * count


def smem():
    return pl.BlockSpec(memory_space=pltpu.SMEM)


def shape(*sizes):
    return jax.ShapeDtypeStruct(sizes, jnp.float32)


def params(collective_id=None):
    if collective_id is None:
        return pltpu.CompilerParams(vmem_limit_bytes=LIMIT)
    return pltpu.CompilerParams(
        collective_id=collective_id, has_side_effects=True, vmem_limit_bytes=LIMIT
    )


def body(
    innovations, block_owner, block_lat, block_lon, block_count,
    error_weight, courant_lon, courant_lat, background_std,
):
    total = lax.axis_size("lat") * lax.axis_size("lon")
    block_total, width = innovations.shape
    levels, columns, latitudes = courant_lon.shape
    rows = latitudes // FOOT
    slots = total * DEPTH
    groups = width // LANES
    wide_rows, wide_columns = rows + 2 * HROW, columns + 2 * HLON
    spot = jnp.pad(
        jnp.repeat(jnp.stack([block_lon, block_lat], axis=1), DEPTH, axis=1).astype(jnp.float32),
        ((0, 0), (0, LANES - 2 * DEPTH)),
    )
    tile = shape(DEPTH, LANES)
    chunks = pltpu.VMEM((total, DEPTH, width), jnp.float32)
    notes = pltpu.VMEM((total, 1, LANES), jnp.float32)
    dma = pltpu.SemaphoreType.DMA

    arrived, anchors, matrix, start, packing, norm, wide = pl.pallas_call(
        first_kernel,
        out_shape=(
            shape(slots, groups, LANES), shape(total, LANES), shape(width, width),
            shape(block_total, width), shape(slots, block_total), tile,
            shape(3, wide_rows, wide_columns, LANES),
        ),
        in_specs=[smem()] + vmem(3) + [pl.BlockSpec(memory_space=pl.ANY)] * 4,
        out_specs=tuple(vmem(7)),
        scratch_shapes=[
            chunks, chunks, notes, notes,
            pltpu.VMEM((width, width), jnp.float32),
            pltpu.VMEM((3, levels, columns, latitudes), jnp.float32),
            *[dma((total,))] * 4, dma((4,)), dma((4,)), dma((4,)),
        ],
        compiler_params=params(0),
    )(block_count, block_owner.reshape(1, block_total), spot, innovations, error_weight[0], courant_lon, courant_lat, background_std)

    corners = anchors[:, : 2 * DEPTH].reshape(total, 2, DEPTH).transpose(1, 0, 2).reshape(-1).astype(jnp.int32)

    def spread(block_rows):
        return pl.pallas_call(
            spread_kernel,
            out_shape=shape(rows + 1, columns, LANES),
            in_specs=[smem()] + vmem(1),
            out_specs=vmem(1)[0],
            compiler_params=params(),
        )(corners, block_rows)

    held = pltpu.VMEM((wide_rows, wide_columns, LANES), jnp.float32)
    first, scaled, model_state, energy = pl.pallas_call(
        system_kernel,
        out_shape=(shape(rows, columns, LANES), shape(rows, columns, LANES), shape(rows + 1, columns, LANES), tile),
        in_specs=vmem(2),
        out_specs=tuple(vmem(4)),
        scratch_shapes=[held, held, dma((4,)), dma((4,))],
        compiler_params=params(1),
    )(spread(arrived), wide)

    picked = pl.pallas_call(
        sample_kernel,
        out_shape=shape(slots, groups, LANES),
        in_specs=[smem()] + vmem(1),
        out_specs=vmem(1)[0],
        compiler_params=params(),
    )(corners, model_state)

    arrived, first_part, direction, step_first, ratio, norm_next, square = pl.pallas_call(
        return_kernel,
        out_shape=(
            shape(slots, groups, LANES), shape(levels, columns, latitudes), shape(block_total, width),
            tile, tile, tile, tile,
        ),
        in_specs=vmem(7),
        out_specs=tuple(vmem(7)),
        scratch_shapes=[chunks] * 4 + [notes] * 4 + [dma((total,))] * 8,
        compiler_params=params(2),
    )(picked, energy, matrix, start, packing, norm, scaled)

    second_part, step_second = pl.pallas_call(
        last_kernel,
        out_shape=(shape(levels, columns, latitudes), tile),
        in_specs=vmem(6),
        out_specs=tuple(vmem(2)),
        scratch_shapes=[held, held, pltpu.VMEM((rows, columns, LANES), jnp.float32), notes, notes, dma((4,)), dma((4,)), dma((total,)), dma((total,))],
        compiler_params=params(3),
    )(spread(arrived), wide, first, ratio, norm_next, square)

    step_first, step_second = step_first[0, 0], step_second[0, 0]
    solution = step_first * start + step_second * direction
    return solution, step_first * first_part + step_second * second_part


def solution(mesh):
    blocks = P(("lat", "lon"))
    in_specs = (
        P(("lat", "lon"), None),
        P(("lat", "lon"), None),
        blocks,
        blocks,
        blocks,
        P(("lat", "lon"), None, None),
        P(None, "lon", "lat"),
        P(None, "lon", "lat"),
        P(None, "lon", "lat"),
    )
    out_specs = (P(("lat", "lon"), None), P(None, "lon", "lat"))
    return jax.shard_map(body, mesh=mesh, in_specs=in_specs, out_specs=out_specs, check_vma=False)
```

```python
import functools

import jax
import jax.numpy as jnp
from jax import lax
from jax.experimental import pallas as pl
from jax.experimental.pallas import tpu as pltpu
from jax.sharding import PartitionSpec as P

FOOT = 4
STEPS = 4
DIFFUSION = 0.15
CENTRE = 1.0 - 4.0 * DIFFUSION
PRECISE = lax.Precision.HIGHEST
MESH = pl.DeviceIdType.MESH
LANES = 128
DEPTH = 8
HLON = 8
HROW = 2
LIMIT = 48 * 1024 * 1024


def place():
    lat_n, lon_n = lax.axis_size("lat"), lax.axis_size("lon")
    lat_i, lon_i = lax.axis_index("lat"), lax.axis_index("lon")
    return lat_n, lon_n, lat_i, lon_i


def signal_all():
    lat_n, lon_n, lat_i, lon_i = place()
    total = lat_n * lon_n
    me = lat_i * lon_n + lon_i
    barrier = pltpu.get_barrier_semaphore()

    def greet(d, carry):
        peer = lax.rem(me + d, total)
        pl.semaphore_signal(
            barrier, inc=1, device_id=(lax.div(peer, lon_n), lax.rem(peer, lon_n)), device_id_type=MESH
        )
        return carry

    lax.fori_loop(1, total, greet, 0)


def wait_all():
    lat_n, lon_n, lat_i, lon_i = place()
    pl.semaphore_wait(pltpu.get_barrier_semaphore(), lat_n * lon_n - 1)


def ways():
    return [(dlat, dlon) for dlat in (-1, 0, 1) for dlon in (-1, 0, 1) if dlat or dlon]


def inside(dlat, lat_i, lat_n):
    return (lat_i + dlat >= 0) & (lat_i + dlat < lat_n)


def signal_near():
    lat_n, lon_n, lat_i, lon_i = place()
    barrier = pltpu.get_barrier_semaphore()
    for dlat, dlon in ways():

        @pl.when(inside(dlat, lat_i, lat_n))
        def _(dlat=dlat, dlon=dlon):
            device = (lat_i + dlat, lax.rem(lon_i + lon_n + dlon, lon_n))
            pl.semaphore_signal(barrier, inc=1, device_id=device, device_id_type=MESH)


def wait_near():
    lat_n, lon_n, lat_i, lon_i = place()
    peers = 2 + jnp.where(lat_i > 0, 3, 0) + jnp.where(lat_i < lat_n - 1, 3, 0)
    pl.semaphore_wait(pltpu.get_barrier_semaphore(), peers)


def trade_copy(sent, got, send_sems, recv_sems, peer, slot, lon_n):
    return pltpu.make_async_remote_copy(
        src_ref=sent.at[peer],
        dst_ref=got.at[slot],
        send_sem=send_sems.at[peer],
        recv_sem=recv_sems.at[slot],
        device_id=(lax.div(peer, lon_n), lax.rem(peer, lon_n)),
        device_id_type=MESH,
    )


def trade_start(sent, got, send_sems, recv_sems):
    lat_n, lon_n, lat_i, lon_i = place()
    total = lat_n * lon_n
    me = lat_i * lon_n + lon_i

    def send(d, carry):
        peer = lax.rem(me + d, total)
        trade_copy(sent, got, send_sems, recv_sems, peer, me, lon_n).start()
        return carry

    lax.fori_loop(1, total, send, 0)
    got[me] = sent[me]


def trade_wait(sent, got, send_sems, recv_sems):
    lat_n, lon_n, lat_i, lon_i = place()
    total = lat_n * lon_n
    me = lat_i * lon_n + lon_i

    def finish(d, carry):
        peer = lax.rem(me + d, total)
        copy = trade_copy(sent, got, send_sems, recv_sems, peer, peer, lon_n)
        copy.wait_send()
        copy.wait_recv()
        return carry

    lax.fori_loop(1, total, finish, 0)


def part(ref, rows, columns):
    if len(ref.shape) == 4:
        return ref.at[:, pl.ds(*rows), pl.ds(*columns)]
    return ref.at[pl.ds(*rows), pl.ds(*columns)]


def halo_copies(wide, send_sems, recv_sems):
    lat_n, lon_n, lat_i, lon_i = place()

    def spans(step, length, halo):
        if step < 0:
            return (halo, halo), (length - halo, halo)
        if step > 0:
            return (length - 2 * halo, halo), (0, halo)
        return (halo, length - 2 * halo), (halo, length - 2 * halo)

    copies = []
    for index, (dlat, dlon) in enumerate(ways()):
        from_rows, to_rows = spans(dlat, wide.shape[-3], HROW)
        from_columns, to_columns = spans(dlon, wide.shape[-2], HLON)
        copy = pltpu.make_async_remote_copy(
            src_ref=part(wide, from_rows, from_columns),
            dst_ref=part(wide, to_rows, to_columns),
            send_sem=send_sems.at[index],
            recv_sem=recv_sems.at[index],
            device_id=(lat_i + dlat, lax.rem(lon_i + lon_n + dlon, lon_n)),
            device_id_type=MESH,
        )
        copies.append((dlat, copy))
    return copies


def halo_start(copies):
    lat_n, lon_n, lat_i, lon_i = place()
    for dlat, copy in copies:

        @pl.when(inside(dlat, lat_i, lat_n))
        def _(copy=copy):
            copy.start()


def halo_wait(copies):
    lat_n, lon_n, lat_i, lon_i = place()
    for dlat, copy in copies:

        @pl.when(inside(dlat, lat_i, lat_n))
        def _(copy=copy):
            copy.wait_send()

        @pl.when(inside(-dlat, lat_i, lat_n))
        def _(copy=copy):
            copy.wait_recv()


def lat_edges(wide):
    lat_n, lon_n, lat_i, lon_i = place()
    rows = wide.shape[-3]
    for ends, first in ((lat_i == 0, 0), (lat_i == lat_n - 1, rows - HROW)):

        @pl.when(ends)
        def _(first=first):
            if len(wide.shape) == 4:
                for index in range(wide.shape[0]):
                    for row in range(HROW):
                        wide[index, first + row] = jnp.zeros(wide.shape[2:], jnp.float32)
            else:
                for row in range(HROW):
                    wide[first + row] = jnp.zeros(wide.shape[1:], jnp.float32)


def dot(left, right, axes=((1,), (0,))):
    return lax.dot_general(
        left, right, (axes, ((), ())), precision=PRECISE, preferred_element_type=jnp.float32
    )


def full_sum(values):
    return jnp.sum(jnp.sum(values, axis=0, keepdims=True), axis=1, keepdims=True)


def gathered_sum(got, lane_index):
    tile = jnp.sum(got[...], axis=0)
    lane = lax.broadcasted_iota(jnp.int32, tile.shape, 1)
    row = lax.broadcasted_iota(jnp.int32, tile.shape, 0)
    return full_sum(jnp.where((lane == lane_index) & (row == 0), tile, 0.0))


def chooser(latitudes):
    rows = latitudes // FOOT
    row = lax.broadcasted_iota(jnp.int32, (latitudes, latitudes), 0)
    column = lax.broadcasted_iota(jnp.int32, (latitudes, latitudes), 1)
    return (column == lax.rem(row, rows) * FOOT + lax.div(row, rows)).astype(jnp.float32)


def regroup(pieces, levels):
    block = lax.div(lax.broadcasted_iota(jnp.int32, pieces[0][0].shape, 1), levels)
    grouped = []
    for i in range(FOOT):
        value = pieces[i][i]
        for q in range(FOOT):
            if q != i:
                moved = pltpu.roll(pieces[q][i], (q - i) % FOOT * levels, 1)
                value = jnp.where(block == q, moved, value)
        grouped.append(value)
    return grouped


def fold(fields, store):
    count, levels, columns, latitudes = fields.shape
    rows = latitudes // FOOT
    choose = chooser(latitudes)

    def group(index, carry):
        for field in range(count):
            stack = jnp.concatenate([fields[field, :, FOOT * index + i, :] for i in range(FOOT)], axis=0)
            mixed = dot(choose, stack, ((1,), (1,)))
            pieces = [[mixed[q * rows : (q + 1) * rows]] * FOOT for q in range(FOOT)]
            for i, value in enumerate(regroup(pieces, levels)):
                store(field, FOOT * index + i, value)
        return carry

    lax.fori_loop(0, columns // FOOT, group, 0, unroll=2)


def unfold(folded, natural):
    levels, columns, latitudes = natural.shape
    choose = chooser(latitudes)

    def group(index, carry):
        planes = [folded[:, FOOT * index + i, :] for i in range(FOOT)]
        mixed = jnp.concatenate(regroup([[plane] * FOOT for plane in planes], levels), axis=0)
        stack = dot(mixed, choose, ((0,), (0,)))
        for i in range(FOOT):
            natural[:, FOOT * index + i, :] = stack[i * levels : (i + 1) * levels]
        return carry

    lax.fori_loop(0, columns // FOOT, group, 0, unroll=5)


def first_kernel(
    count, owner, spot, innovations, matrix, courant_lon, courant_lat, deviation,
    rows_out, anchors_out, permuted, residual, packing, packed_out, norm_out, wide,
    sent, got, note, got_note, held_matrix, held_fields,
    send_sems, recv_sems, note_send, note_recv, halo_send, halo_recv, load_sems,
):
    slots, block_total = packing.shape
    total = slots // DEPTH
    width = matrix.shape[0]
    matrix_copy = pltpu.make_async_copy(matrix, held_matrix, load_sems.at[3])
    matrix_copy.start()
    field_copies = [
        pltpu.make_async_copy(natural, held_fields.at[index], load_sems.at[index])
        for index, natural in enumerate((courant_lon, courant_lat, deviation))
    ]
    for copy in field_copies:
        copy.start()
    lat_edges(wide)
    signal_all()
    matrix_copy.wait()
    live_column = lax.broadcasted_iota(jnp.int32, (block_total, 1), 0) < count[0]
    start = jnp.where(live_column, dot(innovations[...], held_matrix[...], ((1,), (1,))), 0.0)
    residual[...] = start
    row = lax.broadcasted_iota(jnp.int32, (width, width), 0)
    column = lax.broadcasted_iota(jnp.int32, (width, width), 1)
    footprint = FOOT * FOOT
    shuffle = column == lax.rem(row, footprint) * (width // footprint) + lax.div(row, footprint)
    shuffle = shuffle.astype(jnp.float32)
    weighted = dot(dot(start, held_matrix[...]), shuffle)

    live_row = lax.broadcasted_iota(jnp.int32, (1, block_total), 1) < count[0]
    owners = owner[...]
    tiles = lax.broadcasted_iota(jnp.int32, (total, block_total), 0)
    named = jnp.where((tiles == owners) & live_row, 1.0, 0.0)
    earlier = lax.broadcasted_iota(jnp.int32, (block_total, block_total), 0) < lax.broadcasted_iota(
        jnp.int32, (block_total, block_total), 1
    )
    ranks = jnp.sum(named * dot(named, earlier.astype(jnp.float32)), axis=0, keepdims=True)
    target = owners.astype(jnp.float32) * DEPTH + ranks
    slot_ids = lax.broadcasted_iota(jnp.int32, (slots, block_total), 0).astype(jnp.float32)
    pack = jnp.where((slot_ids == target) & live_row, 1.0, 0.0)
    packing[...] = pack
    sent[...] = dot(pack, weighted).reshape(total, DEPTH, width)
    packed_out[...] = sent[...]
    spots = dot(pack, spot[...]).reshape(total, DEPTH, LANES)
    lane = lax.broadcasted_iota(jnp.int32, spots.shape, 2)
    depth = lax.broadcasted_iota(jnp.int32, spots.shape, 1)
    spots = jnp.sum(jnp.where(lax.rem(lane, DEPTH) == depth, spots, 0.0), axis=1, keepdims=True)
    lane = lax.broadcasted_iota(jnp.int32, spots.shape, 2)
    note[...] = jnp.where(lane == 2 * DEPTH, full_sum(start * start)[None], spots)
    wait_all()
    trade_start(sent, got, send_sems, recv_sems)
    trade_start(note, got_note, note_send, note_recv)
    for copy in field_copies:
        copy.wait()

    def store(index, column, value):
        wide[index, pl.ds(HROW, value.shape[0]), HLON + column, :] = value

    fold(held_fields, store)
    copies = halo_copies(wide, halo_send, halo_recv)
    halo_start(copies)
    permuted[...] = dot(held_matrix[...], shuffle)
    trade_wait(sent, got, send_sems, recv_sems)
    trade_wait(note, got_note, note_send, note_recv)
    unload(got, rows_out)
    anchors_out[...] = got_note[...].reshape(total, LANES)
    norm_out[...] = jnp.broadcast_to(gathered_sum(got_note, 2 * DEPTH), norm_out.shape)
    halo_wait(copies)


def unload(got, rows_out):
    slots, groups = rows_out.shape[:2]
    for group in range(groups):
        rows_out[:, group, :] = got[:, :, group * LANES : (group + 1) * LANES].reshape(slots, LANES)


def spread_kernel(anchors, rows, field):
    slots = rows.shape[0]
    level_lanes = LANES // FOOT
    field[...] = jnp.zeros(field.shape, jnp.float32)

    def add(slot, carry):
        column, latitude = anchors[slot], anchors[slots + slot]
        row, shift = lax.div(latitude, FOOT), lax.rem(latitude, FOOT) * level_lanes
        patch = pltpu.roll(rows[slot], shift, 1)
        lane = lax.broadcasted_iota(jnp.int32, patch.shape, 1)
        here = lane >= shift
        field[row, pl.ds(column, FOOT), :] += jnp.where(here, patch, 0.0)
        field[row + 1, pl.ds(column, FOOT), :] += jnp.where(here, 0.0, patch)
        return carry

    lax.fori_loop(0, slots, add, 0, unroll=16)


def sample_kernel(anchors, field, rows):
    slots = rows.shape[0]
    level_lanes = LANES // FOOT

    def pick(slot, carry):
        column, latitude = anchors[slot], anchors[slots + slot]
        row, shift = lax.div(latitude, FOOT), lax.rem(latitude, FOOT) * level_lanes
        here = field[row, pl.ds(column, FOOT), :]
        after = field[row + 1, pl.ds(column, FOOT), :]
        lane = lax.broadcasted_iota(jnp.int32, here.shape, 1)
        rows[slot] = pltpu.roll(jnp.where(lane >= shift, here, after), lax.rem(LANES - shift, LANES), 1)
        return carry

    lax.fori_loop(0, slots, pick, 0, unroll=16)


def model_step(now, later, wide, adjoint):
    lat_n, lon_n, lat_i, lon_i = place()
    rows, columns = now.shape[0], now.shape[1]
    level_lanes = LANES // FOOT
    low = jnp.where(lat_i > 0, 1.0, 0.0)
    high = jnp.where(lat_i < lat_n - 1, 1.0, 0.0)
    lane = lax.broadcasted_iota(jnp.int32, (columns, LANES), 1)
    first, last = lane < level_lanes, lane >= LANES - level_lanes

    def plane(row, carry):
        before, after = lax.rem(row + rows - 1, rows), lax.rem(row + 1, rows)
        here = now[row]
        prior = jnp.where(last, now[before], here)
        following = jnp.where(first, now[after], here)
        zonal, meridional = 0.5 * wide[0, row], wide[1, row]
        if adjoint:
            prior_wind = jnp.where(last, wide[1, before], meridional)
            next_wind = jnp.where(first, wide[1, after], meridional)
            value = (
                CENTRE * here
                + pltpu.roll((DIFFUSION - zonal) * here, 1, 0)
                + pltpu.roll((DIFFUSION + zonal) * here, columns - 1, 0)
                + pltpu.roll((DIFFUSION - 0.5 * prior_wind) * prior, level_lanes, 1)
                + pltpu.roll((DIFFUSION + 0.5 * next_wind) * following, LANES - level_lanes, 1)
            )
        else:
            value = (
                CENTRE * here
                + (DIFFUSION - zonal) * pltpu.roll(here, columns - 1, 0)
                + (DIFFUSION + zonal) * pltpu.roll(here, 1, 0)
                + (DIFFUSION - 0.5 * meridional) * pltpu.roll(following, LANES - level_lanes, 1)
                + (DIFFUSION + 0.5 * meridional) * pltpu.roll(prior, level_lanes, 1)
            )
        keep = jnp.where(row < HROW, low, jnp.where(row >= rows - HROW, high, 1.0))
        later[row] = value * keep
        return carry

    lax.fori_loop(0, rows, plane, 0, unroll=4)


def model_steps(held, other, wide, adjoint):
    def pair(index, carry):
        model_step(held, other, wide, adjoint)
        model_step(other, held, wide, adjoint)
        return carry

    lax.fori_loop(0, STEPS // 2, pair, 0)


def load_wide(field, held, send_sems, recv_sems, signal, wait):
    columns = field.shape[1]
    lat_edges(held)
    signal()

    def fill(row, carry):
        held[HROW + row, pl.ds(HLON, columns)] = field[row]
        return carry

    lax.fori_loop(0, held.shape[0] - 2 * HROW, fill, 0)
    copies = halo_copies(held, send_sems, recv_sems)
    wait()
    halo_start(copies)
    halo_wait(copies)


def system_kernel(
    field, wide_in, adjoint_out, scaled_out, forward_out, energy_out,
    held, other, wide, send_sems, recv_sems, load_sems,
):
    rows, columns = held.shape[0], held.shape[1]
    own = columns - 2 * HLON
    load = pltpu.make_async_copy(wide_in, wide, load_sems.at[0])
    load.start()
    load_wide(field, held, send_sems, recv_sems, signal_near, wait_near)
    load.wait()
    model_steps(held, other, wide, True)

    def scale(row, energy):
        value, deviation = held[row], wide[2, row]
        scaled = deviation * deviation * value
        held[row] = scaled
        adjoint_out[row - HROW] = value[HLON : HLON + own]
        scaled_out[row - HROW] = scaled[HLON : HLON + own]
        return energy + (scaled * value)[HLON : HLON + own]

    energy = lax.fori_loop(HROW, rows - HROW, scale, jnp.zeros((own, LANES), jnp.float32))
    energy_out[...] = jnp.broadcast_to(full_sum(energy), energy_out.shape)
    for row in (*range(HROW), *range(rows - HROW, rows)):
        deviation = wide[2, row]
        held[row] = deviation * deviation * held[row]
    model_steps(held, other, wide, False)

    def write(row, carry):
        forward_out[row] = held[HROW + row, pl.ds(HLON, own)]
        return carry

    lax.fori_loop(0, rows - 2 * HROW, write, 0)
    forward_out[rows - 2 * HROW] = jnp.zeros((own, LANES), jnp.float32)


def return_kernel(
    rows, energy, matrix, start, packing, packed, norm, scaled,
    rows_out, natural_out, direction, step_out, ratio_out, norm_out, square_out,
    sent, got, sent_next, got_next, note, got_note, note_next, got_note_next,
    send_sems, recv_sems, send_next, recv_next, note_send, note_recv, note_send_next, note_recv_next,
):
    slots, groups = rows.shape[:2]
    total = slots // DEPTH
    width = matrix.shape[0]
    signal_all()
    for group in range(groups):
        sent[:, :, group * LANES : (group + 1) * LANES] = rows[:, group, :].reshape(total, DEPTH, LANES)
    note[...] = jnp.broadcast_to(energy[0:1][None], note.shape)
    wait_all()
    trade_start(sent, got, send_sems, recv_sems)
    trade_start(note, got_note, note_send, note_recv)
    product = dot(matrix[...], matrix[...], ((0,), (0,)))
    pack = packing[...]
    filled = jnp.sum(pack, axis=1, keepdims=True) > 0.5
    trade_wait(sent, got, send_sems, recv_sems)
    trade_wait(note, got_note, note_send, note_recv)
    norm_first = norm[0:1, 0:1]
    step = norm_first / (norm_first + gathered_sum(got_note, 0))
    returned = jnp.where(filled, got[...].reshape(slots, width), 0.0)
    change = packed[...].reshape(slots, width) + dot(returned, product)
    sent_next[...] = packed[...] - step * change.reshape(total, DEPTH, width)
    trade_start(sent_next, got_next, send_next, recv_next)
    back = dot(pack, returned, ((0,), (0,)))
    image = start[...] + dot(back, matrix[...], ((1,), (1,)))
    residual = start[...] - step * image
    note_next[...] = jnp.broadcast_to(full_sum(residual * residual)[None], note_next.shape)
    trade_start(note_next, got_note_next, note_send_next, note_recv_next)
    unfold(scaled, natural_out)
    trade_wait(sent_next, got_next, send_next, recv_next)
    trade_wait(note_next, got_note_next, note_send_next, note_recv_next)
    unload(got_next, rows_out)
    norm_next = gathered_sum(got_note_next, 0)
    ratio = norm_next / norm_first
    moved = residual + ratio * start[...]
    direction[...] = moved
    step_out[...] = jnp.broadcast_to(step, step_out.shape)
    ratio_out[...] = jnp.broadcast_to(ratio, ratio_out.shape)
    norm_out[...] = jnp.broadcast_to(norm_next, norm_out.shape)
    square_out[...] = jnp.broadcast_to(full_sum(moved * moved), square_out.shape)


def last_kernel(
    field, wide, earlier, ratio, norm, square,
    natural_out, step_out,
    held, other, scaled, sent, got, halo_send, halo_recv, send_sems, recv_sems,
):
    rows, columns = held.shape[0], held.shape[1]
    own = columns - 2 * HLON
    load_wide(field, held, halo_send, halo_recv, signal_all, wait_all)
    model_steps(held, other, wide, True)
    scale = ratio[0:1, 0:1]

    def combine(row, energy):
        value = held[HROW + row, pl.ds(HLON, own)] + scale * earlier[row]
        deviation = wide[2, HROW + row, pl.ds(HLON, own)]
        product = deviation * deviation * value
        scaled[row] = product
        return energy + product * value

    energy = lax.fori_loop(0, rows - 2 * HROW, combine, jnp.zeros((own, LANES), jnp.float32))
    sent[...] = jnp.broadcast_to((full_sum(energy) + square[0:1, 0:1])[None], sent.shape)
    trade_start(sent, got, send_sems, recv_sems)
    unfold(scaled, natural_out)
    trade_wait(sent, got, send_sems, recv_sems)
    step_out[...] = jnp.broadcast_to(norm[0:1, 0:1] / gathered_sum(got, 0), step_out.shape)


def vmem(count):
    return [pl.BlockSpec(memory_space=pltpu.VMEM)] * count


def hbm(count):
    return [pl.BlockSpec(memory_space=pltpu.HBM)] * count


def smem():
    return pl.BlockSpec(memory_space=pltpu.SMEM)


def shape(*sizes):
    return jax.ShapeDtypeStruct(sizes, jnp.float32)


def params(collective_id=None):
    if collective_id is None:
        return pltpu.CompilerParams(vmem_limit_bytes=LIMIT)
    return pltpu.CompilerParams(
        collective_id=collective_id, has_side_effects=True, vmem_limit_bytes=LIMIT
    )


def body(
    innovations, block_owner, block_lat, block_lon, block_count,
    error_weight, courant_lon, courant_lat, background_std,
):
    total = lax.axis_size("lat") * lax.axis_size("lon")
    block_total, width = innovations.shape
    levels, columns, latitudes = courant_lon.shape
    rows = latitudes // FOOT
    slots = total * DEPTH
    groups = width // LANES
    wide_rows, wide_columns = rows + 2 * HROW, columns + 2 * HLON
    spot = jnp.pad(
        jnp.repeat(jnp.stack([block_lon, block_lat], axis=1), DEPTH, axis=1).astype(jnp.float32),
        ((0, 0), (0, LANES - 2 * DEPTH)),
    )
    tile = shape(DEPTH, LANES)
    chunks = pltpu.VMEM((total, DEPTH, width), jnp.float32)
    notes = pltpu.VMEM((total, 1, LANES), jnp.float32)
    dma = pltpu.SemaphoreType.DMA

    arrived, anchors, matrix, start, packing, packed, norm, wide = pl.pallas_call(
        first_kernel,
        out_shape=(
            shape(slots, groups, LANES), shape(total, LANES), shape(width, width),
            shape(block_total, width), shape(slots, block_total),
            shape(total, DEPTH, width), tile,
            shape(3, wide_rows, wide_columns, LANES),
        ),
        in_specs=[smem()] + vmem(3) + hbm(4),
        out_specs=tuple(vmem(8)),
        scratch_shapes=[
            chunks, chunks, notes, notes,
            pltpu.VMEM((width, width), jnp.float32),
            pltpu.VMEM((3, levels, columns, latitudes), jnp.float32),
            *[dma((total,))] * 4, dma((8,)), dma((8,)), dma((4,)),
        ],
        compiler_params=params(0),
    )(block_count, block_owner.reshape(1, block_total), spot, innovations, error_weight[0], courant_lon, courant_lat, background_std)

    corners = anchors[:, : 2 * DEPTH].reshape(total, 2, DEPTH).transpose(1, 0, 2).reshape(-1).astype(jnp.int32)

    def spread(block_rows):
        return pl.pallas_call(
            spread_kernel,
            out_shape=shape(rows + 1, columns, LANES),
            in_specs=[smem()] + vmem(1),
            out_specs=vmem(1)[0],
            compiler_params=params(),
        )(corners, block_rows)

    held = pltpu.VMEM((wide_rows, wide_columns, LANES), jnp.float32)
    first, scaled, model_state, energy = pl.pallas_call(
        system_kernel,
        out_shape=(shape(rows, columns, LANES), shape(rows, columns, LANES), shape(rows + 1, columns, LANES), tile),
        in_specs=vmem(1) + hbm(1),
        out_specs=tuple(vmem(4)),
        scratch_shapes=[held, held, pltpu.VMEM((3, wide_rows, wide_columns, LANES), jnp.float32), dma((8,)), dma((8,)), dma((1,))],
        compiler_params=params(1),
    )(spread(arrived), wide)

    picked = pl.pallas_call(
        sample_kernel,
        out_shape=shape(slots, groups, LANES),
        in_specs=[smem()] + vmem(1),
        out_specs=vmem(1)[0],
        compiler_params=params(),
    )(corners, model_state)

    arrived, first_part, direction, step_first, ratio, norm_next, square = pl.pallas_call(
        return_kernel,
        out_shape=(
            shape(slots, groups, LANES), shape(levels, columns, latitudes), shape(block_total, width),
            tile, tile, tile, tile,
        ),
        in_specs=vmem(8),
        out_specs=tuple(vmem(7)),
        scratch_shapes=[chunks] * 4 + [notes] * 4 + [dma((total,))] * 8,
        compiler_params=params(2),
    )(picked, energy, matrix, start, packing, packed, norm, scaled)

    second_part, step_second = pl.pallas_call(
        last_kernel,
        out_shape=(shape(levels, columns, latitudes), tile),
        in_specs=vmem(6),
        out_specs=tuple(vmem(2)),
        scratch_shapes=[held, held, pltpu.VMEM((rows, columns, LANES), jnp.float32), notes, notes, dma((8,)), dma((8,)), dma((total,)), dma((total,))],
        compiler_params=params(3),
    )(spread(arrived), wide, first, ratio, norm_next, square)

    step_first, step_second = step_first[0, 0], step_second[0, 0]
    solution = step_first * start + step_second * direction
    return solution, step_first * first_part + step_second * second_part


def solution(mesh):
    blocks = P(("lat", "lon"))
    in_specs = (
        P(("lat", "lon"), None),
        P(("lat", "lon"), None),
        blocks,
        blocks,
        blocks,
        P(("lat", "lon"), None, None),
        P(None, "lon", "lat"),
        P(None, "lon", "lat"),
        P(None, "lon", "lat"),
    )
    out_specs = (P(("lat", "lon"), None), P(None, "lon", "lat"))
    return jax.shard_map(body, mesh=mesh, in_specs=in_specs, out_specs=out_specs, check_vma=False)
```

```python
import functools

import jax
import jax.numpy as jnp
from jax import lax
from jax.experimental import pallas as pl
from jax.experimental.pallas import tpu as pltpu
from jax.sharding import PartitionSpec as P

FOOT = 4
STEPS = 4
DIFFUSION = 0.15
CENTRE = 1.0 - 4.0 * DIFFUSION
PRECISE = lax.Precision.HIGHEST
MESH = pl.DeviceIdType.MESH
LANES = 128
DEPTH = 8
HLON = 8
HROW = 2
LIMIT = 48 * 1024 * 1024


def place():
    lat_n, lon_n = lax.axis_size("lat"), lax.axis_size("lon")
    lat_i, lon_i = lax.axis_index("lat"), lax.axis_index("lon")
    return lat_n, lon_n, lat_i, lon_i


def signal_all():
    lat_n, lon_n, lat_i, lon_i = place()
    total = lat_n * lon_n
    me = lat_i * lon_n + lon_i
    barrier = pltpu.get_barrier_semaphore()

    def greet(d, carry):
        peer = lax.rem(me + d, total)
        pl.semaphore_signal(
            barrier, inc=1, device_id=(lax.div(peer, lon_n), lax.rem(peer, lon_n)), device_id_type=MESH
        )
        return carry

    lax.fori_loop(1, total, greet, 0)


def wait_all():
    lat_n, lon_n, lat_i, lon_i = place()
    pl.semaphore_wait(pltpu.get_barrier_semaphore(), lat_n * lon_n - 1)


def ways():
    return [(dlat, dlon) for dlat in (-1, 0, 1) for dlon in (-1, 0, 1) if dlat or dlon]


def inside(dlat, lat_i, lat_n):
    return (lat_i + dlat >= 0) & (lat_i + dlat < lat_n)


def signal_near():
    lat_n, lon_n, lat_i, lon_i = place()
    barrier = pltpu.get_barrier_semaphore()
    for dlat, dlon in ways():

        @pl.when(inside(dlat, lat_i, lat_n))
        def _(dlat=dlat, dlon=dlon):
            device = (lat_i + dlat, lax.rem(lon_i + lon_n + dlon, lon_n))
            pl.semaphore_signal(barrier, inc=1, device_id=device, device_id_type=MESH)


def wait_near():
    lat_n, lon_n, lat_i, lon_i = place()
    peers = 2 + jnp.where(lat_i > 0, 3, 0) + jnp.where(lat_i < lat_n - 1, 3, 0)
    pl.semaphore_wait(pltpu.get_barrier_semaphore(), peers)


def trade_copy(sent, got, send_sems, recv_sems, peer, slot, lon_n):
    return pltpu.make_async_remote_copy(
        src_ref=sent.at[peer],
        dst_ref=got.at[slot],
        send_sem=send_sems.at[peer],
        recv_sem=recv_sems.at[slot],
        device_id=(lax.div(peer, lon_n), lax.rem(peer, lon_n)),
        device_id_type=MESH,
    )


def trade_start(sent, got, send_sems, recv_sems):
    lat_n, lon_n, lat_i, lon_i = place()
    total = lat_n * lon_n
    me = lat_i * lon_n + lon_i

    def send(d, carry):
        peer = lax.rem(me + d, total)
        trade_copy(sent, got, send_sems, recv_sems, peer, me, lon_n).start()
        return carry

    lax.fori_loop(1, total, send, 0)
    got[me] = sent[me]


def trade_wait(sent, got, send_sems, recv_sems):
    lat_n, lon_n, lat_i, lon_i = place()
    total = lat_n * lon_n
    me = lat_i * lon_n + lon_i

    def finish(d, carry):
        peer = lax.rem(me + d, total)
        copy = trade_copy(sent, got, send_sems, recv_sems, peer, peer, lon_n)
        copy.wait_send()
        copy.wait_recv()
        return carry

    lax.fori_loop(1, total, finish, 0)


def part(ref, rows, columns):
    if len(ref.shape) == 4:
        return ref.at[:, pl.ds(*rows), pl.ds(*columns)]
    return ref.at[pl.ds(*rows), pl.ds(*columns)]


def halo_copies(wide, send_sems, recv_sems):
    lat_n, lon_n, lat_i, lon_i = place()

    def spans(step, length, halo):
        if step < 0:
            return (halo, halo), (length - halo, halo)
        if step > 0:
            return (length - 2 * halo, halo), (0, halo)
        return (halo, length - 2 * halo), (halo, length - 2 * halo)

    copies = []
    for index, (dlat, dlon) in enumerate(ways()):
        from_rows, to_rows = spans(dlat, wide.shape[-3], HROW)
        from_columns, to_columns = spans(dlon, wide.shape[-2], HLON)
        copy = pltpu.make_async_remote_copy(
            src_ref=part(wide, from_rows, from_columns),
            dst_ref=part(wide, to_rows, to_columns),
            send_sem=send_sems.at[index],
            recv_sem=recv_sems.at[index],
            device_id=(lat_i + dlat, lax.rem(lon_i + lon_n + dlon, lon_n)),
            device_id_type=MESH,
        )
        copies.append((dlat, copy))
    return copies


def halo_start(copies):
    lat_n, lon_n, lat_i, lon_i = place()
    for dlat, copy in copies:

        @pl.when(inside(dlat, lat_i, lat_n))
        def _(copy=copy):
            copy.start()


def halo_wait(copies):
    lat_n, lon_n, lat_i, lon_i = place()
    for dlat, copy in copies:

        @pl.when(inside(dlat, lat_i, lat_n))
        def _(copy=copy):
            copy.wait_send()

        @pl.when(inside(-dlat, lat_i, lat_n))
        def _(copy=copy):
            copy.wait_recv()


def lat_edges(wide):
    lat_n, lon_n, lat_i, lon_i = place()
    rows = wide.shape[-3]
    for ends, first in ((lat_i == 0, 0), (lat_i == lat_n - 1, rows - HROW)):

        @pl.when(ends)
        def _(first=first):
            if len(wide.shape) == 4:
                for index in range(wide.shape[0]):
                    for row in range(HROW):
                        wide[index, first + row] = jnp.zeros(wide.shape[2:], jnp.float32)
            else:
                for row in range(HROW):
                    wide[first + row] = jnp.zeros(wide.shape[1:], jnp.float32)


def dot(left, right, axes=((1,), (0,))):
    return lax.dot_general(
        left, right, (axes, ((), ())), precision=PRECISE, preferred_element_type=jnp.float32
    )


def full_sum(values):
    return jnp.sum(jnp.sum(values, axis=0, keepdims=True), axis=1, keepdims=True)


def gathered_sum(got, lane_index):
    tile = jnp.sum(got[...], axis=0)
    lane = lax.broadcasted_iota(jnp.int32, tile.shape, 1)
    row = lax.broadcasted_iota(jnp.int32, tile.shape, 0)
    return full_sum(jnp.where((lane == lane_index) & (row == 0), tile, 0.0))


def chooser(latitudes):
    rows = latitudes // FOOT
    row = lax.broadcasted_iota(jnp.int32, (latitudes, latitudes), 0)
    column = lax.broadcasted_iota(jnp.int32, (latitudes, latitudes), 1)
    return (column == lax.rem(row, rows) * FOOT + lax.div(row, rows)).astype(jnp.float32)


def regroup(pieces, levels):
    block = lax.div(lax.broadcasted_iota(jnp.int32, pieces[0][0].shape, 1), levels)
    grouped = []
    for i in range(FOOT):
        value = pieces[i][i]
        for q in range(FOOT):
            if q != i:
                moved = pltpu.roll(pieces[q][i], (q - i) % FOOT * levels, 1)
                value = jnp.where(block == q, moved, value)
        grouped.append(value)
    return grouped


def fold(fields, store):
    count, levels, columns, latitudes = fields.shape
    rows = latitudes // FOOT
    choose = chooser(latitudes)

    def group(index, carry):
        for field in range(count):
            stack = jnp.concatenate([fields[field, :, FOOT * index + i, :] for i in range(FOOT)], axis=0)
            mixed = dot(choose, stack, ((1,), (1,)))
            pieces = [[mixed[q * rows : (q + 1) * rows]] * FOOT for q in range(FOOT)]
            for i, value in enumerate(regroup(pieces, levels)):
                store(field, FOOT * index + i, value)
        return carry

    lax.fori_loop(0, columns // FOOT, group, 0, unroll=2)


def unfold(folded, natural):
    levels, columns, latitudes = natural.shape
    choose = chooser(latitudes)

    def group(index, carry):
        planes = [folded[:, FOOT * index + i, :] for i in range(FOOT)]
        mixed = jnp.concatenate(regroup([[plane] * FOOT for plane in planes], levels), axis=0)
        stack = dot(mixed, choose, ((0,), (0,)))
        for i in range(FOOT):
            natural[:, FOOT * index + i, :] = stack[i * levels : (i + 1) * levels]
        return carry

    lax.fori_loop(0, columns // FOOT, group, 0, unroll=5)


def first_kernel(
    count, owner, spot, innovations, matrix, courant_lon, courant_lat, deviation,
    rows_out, anchors_out, permuted, residual, packing, packed_out, norm_out, wide,
    sent, got, note, got_note, held_matrix, held_fields,
    send_sems, recv_sems, note_send, note_recv, halo_send, halo_recv, load_sems,
):
    slots, block_total = packing.shape
    total = slots // DEPTH
    width = matrix.shape[0]
    matrix_copy = pltpu.make_async_copy(matrix, held_matrix, load_sems.at[3])
    matrix_copy.start()
    field_copies = [
        pltpu.make_async_copy(natural, held_fields.at[index], load_sems.at[index])
        for index, natural in enumerate((courant_lon, courant_lat, deviation))
    ]
    for copy in field_copies:
        copy.start()
    lat_edges(wide)
    signal_all()
    matrix_copy.wait()
    live_column = lax.broadcasted_iota(jnp.int32, (block_total, 1), 0) < count[0]
    start = jnp.where(live_column, dot(innovations[...], held_matrix[...], ((1,), (1,))), 0.0)
    residual[...] = start
    row = lax.broadcasted_iota(jnp.int32, (width, width), 0)
    column = lax.broadcasted_iota(jnp.int32, (width, width), 1)
    footprint = FOOT * FOOT
    shuffle = column == lax.rem(row, footprint) * (width // footprint) + lax.div(row, footprint)
    shuffle = shuffle.astype(jnp.float32)
    weighted = dot(dot(start, held_matrix[...]), shuffle)

    live_row = lax.broadcasted_iota(jnp.int32, (1, block_total), 1) < count[0]
    owners = owner[...]
    tiles = lax.broadcasted_iota(jnp.int32, (total, block_total), 0)
    named = jnp.where((tiles == owners) & live_row, 1.0, 0.0)
    earlier = lax.broadcasted_iota(jnp.int32, (block_total, block_total), 0) < lax.broadcasted_iota(
        jnp.int32, (block_total, block_total), 1
    )
    ranks = jnp.sum(named * dot(named, earlier.astype(jnp.float32)), axis=0, keepdims=True)
    target = owners.astype(jnp.float32) * DEPTH + ranks
    slot_ids = lax.broadcasted_iota(jnp.int32, (slots, block_total), 0).astype(jnp.float32)
    pack = jnp.where((slot_ids == target) & live_row, 1.0, 0.0)
    packing[...] = pack
    sent[...] = dot(pack, weighted).reshape(total, DEPTH, width)
    packed_out[...] = sent[...]
    spots = dot(pack, spot[...]).reshape(total, DEPTH, LANES)
    lane = lax.broadcasted_iota(jnp.int32, spots.shape, 2)
    depth = lax.broadcasted_iota(jnp.int32, spots.shape, 1)
    spots = jnp.sum(jnp.where(lax.rem(lane, DEPTH) == depth, spots, 0.0), axis=1, keepdims=True)
    lane = lax.broadcasted_iota(jnp.int32, spots.shape, 2)
    note[...] = jnp.where(lane == 2 * DEPTH, full_sum(start * start)[None], spots)
    wait_all()
    trade_start(sent, got, send_sems, recv_sems)
    trade_start(note, got_note, note_send, note_recv)
    for copy in field_copies:
        copy.wait()

    def store(index, column, value):
        wide[index, pl.ds(HROW, value.shape[0]), HLON + column, :] = value

    fold(held_fields, store)
    copies = halo_copies(wide, halo_send, halo_recv)
    halo_start(copies)
    permuted[...] = dot(held_matrix[...], shuffle)
    trade_wait(sent, got, send_sems, recv_sems)
    trade_wait(note, got_note, note_send, note_recv)
    unload(got, rows_out)
    anchors_out[...] = got_note[...].reshape(total, LANES)
    norm_out[...] = jnp.broadcast_to(gathered_sum(got_note, 2 * DEPTH), norm_out.shape)
    halo_wait(copies)


def unload(got, rows_out):
    slots, groups = rows_out.shape[:2]
    for group in range(groups):
        rows_out[:, group, :] = got[:, :, group * LANES : (group + 1) * LANES].reshape(slots, LANES)


def spread_kernel(anchors, rows, field):
    slots = rows.shape[0]
    level_lanes = LANES // FOOT
    field[...] = jnp.zeros(field.shape, jnp.float32)

    def add(slot, carry):
        column, latitude = anchors[slot], anchors[slots + slot]
        row, shift = lax.div(latitude, FOOT), lax.rem(latitude, FOOT) * level_lanes
        patch = pltpu.roll(rows[slot], shift, 1)
        lane = lax.broadcasted_iota(jnp.int32, patch.shape, 1)
        here = lane >= shift
        field[row, pl.ds(column, FOOT), :] += jnp.where(here, patch, 0.0)
        field[row + 1, pl.ds(column, FOOT), :] += jnp.where(here, 0.0, patch)
        return carry

    lax.fori_loop(0, slots, add, 0, unroll=16)


def sample_kernel(anchors, field, rows):
    slots = rows.shape[0]
    level_lanes = LANES // FOOT

    def pick(slot, carry):
        column, latitude = anchors[slot], anchors[slots + slot]
        row, shift = lax.div(latitude, FOOT), lax.rem(latitude, FOOT) * level_lanes
        here = field[row, pl.ds(column, FOOT), :]
        after = field[row + 1, pl.ds(column, FOOT), :]
        lane = lax.broadcasted_iota(jnp.int32, here.shape, 1)
        rows[slot] = pltpu.roll(jnp.where(lane >= shift, here, after), lax.rem(LANES - shift, LANES), 1)
        return carry

    lax.fori_loop(0, slots, pick, 0, unroll=16)


def model_step(now, later, wide, adjoint):
    lat_n, lon_n, lat_i, lon_i = place()
    rows, columns = now.shape[0], now.shape[1]
    level_lanes = LANES // FOOT
    low = jnp.where(lat_i > 0, 1.0, 0.0)
    high = jnp.where(lat_i < lat_n - 1, 1.0, 0.0)
    lane = lax.broadcasted_iota(jnp.int32, (columns, LANES), 1)
    first, last = lane < level_lanes, lane >= LANES - level_lanes

    def plane(row, carry):
        before, after = lax.rem(row + rows - 1, rows), lax.rem(row + 1, rows)
        here = now[row]
        prior = jnp.where(last, now[before], here)
        following = jnp.where(first, now[after], here)
        zonal, meridional = 0.5 * wide[0, row], wide[1, row]
        if adjoint:
            prior_wind = jnp.where(last, wide[1, before], meridional)
            next_wind = jnp.where(first, wide[1, after], meridional)
            value = (
                CENTRE * here
                + pltpu.roll((DIFFUSION - zonal) * here, 1, 0)
                + pltpu.roll((DIFFUSION + zonal) * here, columns - 1, 0)
                + pltpu.roll((DIFFUSION - 0.5 * prior_wind) * prior, level_lanes, 1)
                + pltpu.roll((DIFFUSION + 0.5 * next_wind) * following, LANES - level_lanes, 1)
            )
        else:
            value = (
                CENTRE * here
                + (DIFFUSION - zonal) * pltpu.roll(here, columns - 1, 0)
                + (DIFFUSION + zonal) * pltpu.roll(here, 1, 0)
                + (DIFFUSION - 0.5 * meridional) * pltpu.roll(following, LANES - level_lanes, 1)
                + (DIFFUSION + 0.5 * meridional) * pltpu.roll(prior, level_lanes, 1)
            )
        keep = jnp.where(row < HROW, low, jnp.where(row >= rows - HROW, high, 1.0))
        later[row] = value * keep
        return carry

    lax.fori_loop(0, rows, plane, 0, unroll=4)


def model_steps(held, other, wide, adjoint):
    def pair(index, carry):
        model_step(held, other, wide, adjoint)
        model_step(other, held, wide, adjoint)
        return carry

    lax.fori_loop(0, STEPS // 2, pair, 0)


def load_wide(field, held, send_sems, recv_sems, signal, wait):
    columns = field.shape[1]
    lat_edges(held)
    signal()

    def fill(row, carry):
        held[HROW + row, pl.ds(HLON, columns)] = field[row]
        return carry

    lax.fori_loop(0, held.shape[0] - 2 * HROW, fill, 0)
    copies = halo_copies(held, send_sems, recv_sems)
    wait()
    halo_start(copies)
    halo_wait(copies)


def system_kernel(
    field, wide_in, adjoint_out, scaled_out, forward_out, energy_out,
    held, other, wide, send_sems, recv_sems, load_sems,
):
    rows, columns = held.shape[0], held.shape[1]
    own = columns - 2 * HLON
    load = pltpu.make_async_copy(wide_in, wide, load_sems.at[0])
    load.start()
    load_wide(field, held, send_sems, recv_sems, signal_near, wait_near)
    load.wait()
    model_steps(held, other, wide, True)

    def scale(row, energy):
        value, deviation = held[row], wide[2, row]
        scaled = deviation * deviation * value
        held[row] = scaled
        adjoint_out[row - HROW] = value[HLON : HLON + own]
        scaled_out[row - HROW] = scaled[HLON : HLON + own]
        return energy + (scaled * value)[HLON : HLON + own]

    energy = lax.fori_loop(HROW, rows - HROW, scale, jnp.zeros((own, LANES), jnp.float32))
    energy_out[...] = jnp.broadcast_to(full_sum(energy), energy_out.shape)
    for row in (*range(HROW), *range(rows - HROW, rows)):
        deviation = wide[2, row]
        held[row] = deviation * deviation * held[row]
    model_steps(held, other, wide, False)

    def write(row, carry):
        forward_out[row] = held[HROW + row, pl.ds(HLON, own)]
        return carry

    lax.fori_loop(0, rows - 2 * HROW, write, 0)
    forward_out[rows - 2 * HROW] = jnp.zeros((own, LANES), jnp.float32)


def return_kernel(
    rows, energy, matrix, start, packing, packed, norm, scaled,
    rows_out, natural_out, direction, step_out, ratio_out, norm_out, square_out,
    sent, got, sent_next, got_next, note, got_note, note_next, got_note_next,
    send_sems, recv_sems, send_next, recv_next, note_send, note_recv, note_send_next, note_recv_next,
):
    slots, groups = rows.shape[:2]
    total = slots // DEPTH
    width = matrix.shape[0]
    signal_all()
    for group in range(groups):
        sent[:, :, group * LANES : (group + 1) * LANES] = rows[:, group, :].reshape(total, DEPTH, LANES)
    note[...] = jnp.broadcast_to(energy[0:1][None], note.shape)
    wait_all()
    trade_start(sent, got, send_sems, recv_sems)
    trade_start(note, got_note, note_send, note_recv)
    product = dot(matrix[...], matrix[...], ((0,), (0,)))
    pack = packing[...]
    filled = jnp.sum(pack, axis=1, keepdims=True) > 0.5
    trade_wait(sent, got, send_sems, recv_sems)
    trade_wait(note, got_note, note_send, note_recv)
    norm_first = norm[0:1, 0:1]
    step = norm_first / (norm_first + gathered_sum(got_note, 0))
    returned = jnp.where(filled, got[...].reshape(slots, width), 0.0)
    change = packed[...].reshape(slots, width) + dot(returned, product)
    sent_next[...] = packed[...] - step * change.reshape(total, DEPTH, width)
    trade_start(sent_next, got_next, send_next, recv_next)
    back = dot(pack, returned, ((0,), (0,)))
    image = start[...] + dot(back, matrix[...], ((1,), (1,)))
    residual = start[...] - step * image
    note_next[...] = jnp.broadcast_to(full_sum(residual * residual)[None], note_next.shape)
    trade_start(note_next, got_note_next, note_send_next, note_recv_next)
    unfold(scaled, natural_out)
    trade_wait(sent_next, got_next, send_next, recv_next)
    trade_wait(note_next, got_note_next, note_send_next, note_recv_next)
    unload(got_next, rows_out)
    norm_next = gathered_sum(got_note_next, 0)
    ratio = norm_next / norm_first
    moved = residual + ratio * start[...]
    direction[...] = moved
    step_out[...] = jnp.broadcast_to(step, step_out.shape)
    ratio_out[...] = jnp.broadcast_to(ratio, ratio_out.shape)
    norm_out[...] = jnp.broadcast_to(norm_next, norm_out.shape)
    square_out[...] = jnp.broadcast_to(full_sum(moved * moved), square_out.shape)


def last_kernel(
    field, wide, earlier, ratio, norm, square,
    natural_out, step_out,
    held, other, scaled, sent, got, halo_send, halo_recv, send_sems, recv_sems,
):
    rows, columns = held.shape[0], held.shape[1]
    own = columns - 2 * HLON
    load_wide(field, held, halo_send, halo_recv, signal_all, wait_all)
    model_steps(held, other, wide, True)
    scale = ratio[0:1, 0:1]

    def combine(row, energy):
        value = held[HROW + row, pl.ds(HLON, own)] + scale * earlier[row]
        deviation = wide[2, HROW + row, pl.ds(HLON, own)]
        product = deviation * deviation * value
        scaled[row] = product
        return energy + product * value

    energy = lax.fori_loop(0, rows - 2 * HROW, combine, jnp.zeros((own, LANES), jnp.float32))
    sent[...] = jnp.broadcast_to((full_sum(energy) + square[0:1, 0:1])[None], sent.shape)
    trade_start(sent, got, send_sems, recv_sems)
    unfold(scaled, natural_out)
    trade_wait(sent, got, send_sems, recv_sems)
    step_out[...] = jnp.broadcast_to(norm[0:1, 0:1] / gathered_sum(got, 0), step_out.shape)


def vmem(count):
    return [pl.BlockSpec(memory_space=pltpu.VMEM)] * count


def hbm(count):
    return [pl.BlockSpec(memory_space=pltpu.HBM)] * count


def smem():
    return pl.BlockSpec(memory_space=pltpu.SMEM)


def shape(*sizes):
    return jax.ShapeDtypeStruct(sizes, jnp.float32)


def params(collective_id=None, limit=LIMIT):
    if collective_id is None:
        return pltpu.CompilerParams(vmem_limit_bytes=LIMIT)
    return pltpu.CompilerParams(
        collective_id=collective_id, has_side_effects=True, vmem_limit_bytes=limit
    )


def body(
    innovations, block_owner, block_lat, block_lon, block_count,
    error_weight, courant_lon, courant_lat, background_std,
):
    total = lax.axis_size("lat") * lax.axis_size("lon")
    block_total, width = innovations.shape
    levels, columns, latitudes = courant_lon.shape
    rows = latitudes // FOOT
    slots = total * DEPTH
    groups = width // LANES
    wide_rows, wide_columns = rows + 2 * HROW, columns + 2 * HLON
    spot = jnp.pad(
        jnp.repeat(jnp.stack([block_lon, block_lat], axis=1), DEPTH, axis=1).astype(jnp.float32),
        ((0, 0), (0, LANES - 2 * DEPTH)),
    )
    tile = shape(DEPTH, LANES)
    chunks = pltpu.VMEM((total, DEPTH, width), jnp.float32)
    notes = pltpu.VMEM((total, 1, LANES), jnp.float32)
    dma = pltpu.SemaphoreType.DMA

    arrived, anchors, matrix, start, packing, packed, norm, wide = pl.pallas_call(
        first_kernel,
        out_shape=(
            shape(slots, groups, LANES), shape(total, LANES), shape(width, width),
            shape(block_total, width), shape(slots, block_total),
            shape(total, DEPTH, width), tile,
            shape(3, wide_rows, wide_columns, LANES),
        ),
        in_specs=[smem()] + vmem(3) + hbm(4),
        out_specs=tuple(vmem(8)),
        scratch_shapes=[
            chunks, chunks, notes, notes,
            pltpu.VMEM((width, width), jnp.float32),
            pltpu.VMEM((3, levels, columns, latitudes), jnp.float32),
            *[dma((total,))] * 4, dma((8,)), dma((8,)), dma((4,)),
        ],
        compiler_params=params(0, 60 * 1024 * 1024),
    )(block_count, block_owner.reshape(1, block_total), spot, innovations, error_weight[0], courant_lon, courant_lat, background_std)

    corners = anchors[:, : 2 * DEPTH].reshape(total, 2, DEPTH).transpose(1, 0, 2).reshape(-1).astype(jnp.int32)

    def spread(block_rows):
        return pl.pallas_call(
            spread_kernel,
            out_shape=shape(rows + 1, columns, LANES),
            in_specs=[smem()] + vmem(1),
            out_specs=vmem(1)[0],
            compiler_params=params(),
        )(corners, block_rows)

    held = pltpu.VMEM((wide_rows, wide_columns, LANES), jnp.float32)
    first, scaled, model_state, energy = pl.pallas_call(
        system_kernel,
        out_shape=(shape(rows, columns, LANES), shape(rows, columns, LANES), shape(rows + 1, columns, LANES), tile),
        in_specs=vmem(1) + hbm(1),
        out_specs=tuple(vmem(4)),
        scratch_shapes=[held, held, pltpu.VMEM((3, wide_rows, wide_columns, LANES), jnp.float32), dma((8,)), dma((8,)), dma((1,))],
        compiler_params=params(1),
    )(spread(arrived), wide)

    picked = pl.pallas_call(
        sample_kernel,
        out_shape=shape(slots, groups, LANES),
        in_specs=[smem()] + vmem(1),
        out_specs=vmem(1)[0],
        compiler_params=params(),
    )(corners, model_state)

    arrived, first_part, direction, step_first, ratio, norm_next, square = pl.pallas_call(
        return_kernel,
        out_shape=(
            shape(slots, groups, LANES), shape(levels, columns, latitudes), shape(block_total, width),
            tile, tile, tile, tile,
        ),
        in_specs=vmem(8),
        out_specs=tuple(vmem(7)),
        scratch_shapes=[chunks] * 4 + [notes] * 4 + [dma((total,))] * 8,
        compiler_params=params(2),
    )(picked, energy, matrix, start, packing, packed, norm, scaled)

    second_part, step_second = pl.pallas_call(
        last_kernel,
        out_shape=(shape(levels, columns, latitudes), tile),
        in_specs=vmem(6),
        out_specs=tuple(vmem(2)),
        scratch_shapes=[held, held, pltpu.VMEM((rows, columns, LANES), jnp.float32), notes, notes, dma((8,)), dma((8,)), dma((total,)), dma((total,))],
        compiler_params=params(3),
    )(spread(arrived), wide, first, ratio, norm_next, square)

    step_first, step_second = step_first[0, 0], step_second[0, 0]
    solution = step_first * start + step_second * direction
    return solution, step_first * first_part + step_second * second_part


def solution(mesh):
    blocks = P(("lat", "lon"))
    in_specs = (
        P(("lat", "lon"), None),
        P(("lat", "lon"), None),
        blocks,
        blocks,
        blocks,
        P(("lat", "lon"), None, None),
        P(None, "lon", "lat"),
        P(None, "lon", "lat"),
        P(None, "lon", "lat"),
    )
    out_specs = (P(("lat", "lon"), None), P(None, "lon", "lat"))
    return jax.shard_map(body, mesh=mesh, in_specs=in_specs, out_specs=out_specs, check_vma=False)
```
